32 devices in a mesh: azim: 4 (over z), beam: 2 (over y), sweep: 4 (over x, core).
Axes of the slice: x: 2, y: 2, z: 4, core: 2. Of those that a mesh axis runs over, the one named last changes fastest.
Arguments:
- features: bfloat16 [256, 4, 4, 256], P('azim', 'sweep', 'beam'), may hold values from -16 to 16
- cotangent: bfloat16 [256, 4, 4, 256], P('azim', 'sweep', 'beam'), may hold values from -6 to 6
- w_query: bfloat16 [256, 256], replicated
- w_key: bfloat16 [256, 256], replicated
- w_value: bfloat16 [256, 256], replicated, may hold values from -0.375 to 0.375
- w_out: bfloat16 [256, 256], replicated, may hold values from -0.375 to 0.375
- w_conv: bfloat16 [256, 27, 256], replicated, may hold values from -0.078125 to 0.078125
- sector_mask: int32 [4, 4], replicated, may hold values from 0 to 1, as said below
Outputs:
- features_grad: bfloat16 [256, 4, 4, 256], P('azim', 'sweep', 'beam')
- weight_grads: float32 [256, 31, 256], P('azim', None, ('beam', 'sweep'))
The draws below stay inside these ranges and needn't reach their ends.
Inputs may be any that keep to these rules, and one draw needn't show every extreme that they name: `sector_mask`: entry [i, j] is 1 where query sector i may attend to key sector j, else 0; every diagonal entry is 1.
All inputs are finite; a program needn't handle non-finite values.
Results may differ from the reference program's by a relative error of at most 0.012.
The reference program's roundings to bfloat16 on the way count: a program that leaves them out, or rounds other values in their place, can miss the bound.
Values may be sent and summed in bfloat16 or wider, within the bound.
No kernel may reach another device: no remote copies, remote signals or barrier semaphores. Data moves between devices by JAX's collectives and lax.ppermute only.
A program may use at most 128 MiB of HBM per device.

```python
import jax
import jax.numpy as jnp
from jax import lax

D = 256
HEADS = 8
SECTOR = 64
TAPS = 27
NAZ = 256
NSW = 4
NBM = 4
SECTORS = 4


def draw_features(key, part):
    extent = (NAZ, NSW, NBM, D)
    subkeys = jax.random.split(key, 1)
    return jnp.clip(jax.random.normal(subkeys[0], extent, jnp.float32), -6.0, 6.0).astype(jnp.bfloat16)


def projection_pair(key):
    first_key, second_key = jax.random.split(jax.random.fold_in(key, 11))
    spread = D ** (-0.5)
    query_part = jnp.clip(jax.random.normal(first_key, (D, D), jnp.float32), -3.0, 3.0) * spread
    other_part = jnp.clip(jax.random.normal(second_key, (D, D), jnp.float32), -3.0, 3.0) * spread
    return (query_part, other_part)


def draw_w_query(key, part):
    return projection_pair(key)[0].astype(jnp.bfloat16)


def draw_w_key(key, part):
    return projection_pair(key)[1].astype(jnp.bfloat16)


def draw_sector_mask(key, part):
    first_key, second_key = jax.random.split(jax.random.fold_in(key, 23))
    row_rates = jax.random.randint(first_key, (SECTORS, 1), 15, 90)
    dice_rolls = jax.random.randint(second_key, (SECTORS, SECTORS), 0, 100)
    diagonal = jnp.arange(SECTORS)[:, None] == jnp.arange(SECTORS)[None, :]
    return jnp.where(diagonal, 1, (dice_rolls < row_rates).astype(jnp.int32)).astype(jnp.int32)


def level_of(own_key, dims, cuts, low, largest):
    loudness = 1.0
    for position, parts in cuts:
        heights = jax.random.uniform(jax.random.fold_in(jax.random.fold_in(own_key, 6), position), (parts,), jnp.float32, low / len(cuts), largest / len(cuts))
        loudness = loudness * jnp.repeat(jnp.exp(heights), dims[position] // parts).reshape((-1,) + (1,) * (len(dims) - 1 - position))
    return loudness


def centred(rng, dims, width, reach, pieces=(), kind=jnp.bfloat16):
    level = level_of(rng, dims, pieces, -0.22, 0.18) if pieces else 1.0
    array = jax.random.normal(rng, dims, jnp.float32) * width * level
    return jnp.minimum(jnp.maximum(array, -reach), reach).astype(kind)


def setup_inputs(seed: int = 0) -> dict:
    splits = jax.random.split(jax.random.key(seed), 9)
    return {
        "features": draw_features(jax.random.fold_in(splits[8], 71), 0),
        "cotangent": centred(splits[1], (NAZ, NSW, NBM, D), 1.0, 6.0, ((0, 4), (1, 4), (2, 2))),
        "w_query": draw_w_query(jax.random.fold_in(splits[8], 71), 0),
        "w_key": draw_w_key(jax.random.fold_in(splits[8], 71), 0),
        "w_value": centred(splits[4], (D, D), D ** -0.5, 0.375),
        "w_out": centred(splits[5], (D, D), D ** -0.5, 0.375),
        "w_conv": centred(splits[6], (D, TAPS, D), (TAPS * D) ** -0.5, 0.078125),
        "sector_mask": draw_sector_mask(jax.random.fold_in(splits[8], 71), 0),
    }


highest = lax.Precision.HIGHEST
masked_score = -1e30


def matmul(left_side, right_side):
    return jnp.dot(left_side.astype(jnp.float32), right_side.astype(jnp.float32), precision=highest)


def rounded(tensor):
    return lax.optimization_barrier(tensor.astype(jnp.bfloat16)).astype(jnp.float32)


def pad_grid(grid_in):
    wrapped = jnp.concatenate([grid_in[-1:], grid_in, grid_in[:1]], axis=0)
    return jnp.pad(wrapped, ((0, 0), (1, 1), (1, 1), (0, 0)))


def reference(features, cotangent, w_query, w_key, w_value, w_out, w_conv, sector_mask):
    extent = features.shape
    col_count, sweeps, beam_rows, channels = extent
    tokens = col_count * sweeps * beam_rows
    sequences = sweeps * beam_rows
    head_size = channels // HEADS
    score_scale = head_size ** -0.5
    flat_in = features.astype(jnp.float32).reshape(tokens, channels)
    queries = rounded(matmul(flat_in, w_query))
    key_proj = rounded(matmul(flat_in, w_key))
    values = rounded(matmul(flat_in, w_value))
    allowed = jnp.repeat(jnp.repeat(sector_mask, SECTOR, axis=0), SECTOR, axis=1) > 0

    def by_sequence(tensor):
        return tensor.reshape(col_count, sequences, HEADS, head_size).transpose(1, 0, 2, 3)

    def by_token(tensor):
        return tensor.transpose(1, 0, 2, 3).reshape(tokens, channels)

    def scores_of(query_seq, key_seq):
        raw_scores = jnp.einsum("ahe,khe->hak", query_seq, key_seq, precision=highest)
        return jnp.where(allowed, raw_scores * score_scale, masked_score)

    def forward_one(operands):
        query_seq, key_seq, value_seq = operands
        scores = scores_of(query_seq, key_seq)
        peak_score = jnp.max(scores, axis=-1)
        logsum = peak_score + jnp.log(jnp.sum(jnp.exp(scores - peak_score[..., None]), axis=-1))
        weights_full = jnp.where(allowed, jnp.exp(scores - logsum[..., None]), 0.0)
        attended_one = rounded(jnp.einsum("hak,khe->ahe", rounded(weights_full), value_seq, precision=highest))
        return attended_one, logsum

    attended_seq, logsum_seq = lax.map(forward_one, (by_sequence(queries), by_sequence(key_proj), by_sequence(values)))
    attended = by_token(attended_seq)
    layer_out = rounded(flat_in + matmul(attended, w_out))
    layer_pad = pad_grid(layer_out.reshape(extent).astype(jnp.bfloat16))
    cot_pad = pad_grid(cotangent)
    cot_flat = cotangent.astype(jnp.float32).reshape(tokens, channels)
    grad_layer = cot_flat
    conv_grads = []
    for offset_one in (-1, 0, 1):
        for offset_two in (-1, 0, 1):
            for offset_three in (-1, 0, 1):
                tap_index = 9 * (offset_one + 1) + 3 * (offset_two + 1) + (offset_three + 1)
                cot_piece = cot_pad[1 - offset_one:1 - offset_one + col_count, 1 - offset_two:1 - offset_two + sweeps, 1 - offset_three:1 - offset_three + beam_rows]
                layer_piece = layer_pad[1 + offset_one:1 + offset_one + col_count, 1 + offset_two:1 + offset_two + sweeps, 1 + offset_three:1 + offset_three + beam_rows]
                grad_layer = grad_layer + matmul(cot_piece.reshape(tokens, channels), w_conv[:, tap_index, :].T)
                conv_grads.append(matmul(layer_piece.reshape(tokens, channels).T, cot_flat))
    grad_layer_bf = rounded(grad_layer)
    grad_attended = rounded(matmul(grad_layer_bf, w_out.T))

    def backward_one(operands):
        query_seq, key_seq, value_seq, attended_one, grad_one, logsum = operands
        scores = scores_of(query_seq, key_seq)
        weights_full = jnp.where(allowed, jnp.exp(scores - logsum[..., None]), 0.0)
        row_delta = jnp.einsum("ahe,ahe->ha", grad_one, attended_one, precision=highest)
        grad_prob = jnp.einsum("ahe,khe->hak", grad_one, value_seq, precision=highest)
        grad_score = rounded(weights_full * (grad_prob - row_delta[..., None]))
        grad_query_one = jnp.einsum("hak,khe->ahe", grad_score, key_seq, precision=highest) * score_scale
        grad_key_one = jnp.einsum("hak,ahe->khe", grad_score, query_seq, precision=highest) * score_scale
        grad_value_one = jnp.einsum("hak,ahe->khe", rounded(weights_full), grad_one, precision=highest)
        return grad_query_one, grad_key_one, grad_value_one

    grad_query_seq, grad_key_seq, grad_value_seq = lax.map(backward_one, (by_sequence(queries), by_sequence(key_proj), by_sequence(values), attended_seq, by_sequence(grad_attended), logsum_seq))
    grad_query = by_token(grad_query_seq)
    grad_key = by_token(grad_key_seq)
    grad_value = by_token(grad_value_seq)
    grad_in = grad_layer + matmul(grad_query, w_query.T) + matmul(grad_key, w_key.T) + matmul(grad_value, w_value.T)
    features_grad = grad_in.astype(jnp.bfloat16).reshape(extent)
    projection_grads = jnp.stack([matmul(flat_in.T, grad_query), matmul(flat_in.T, grad_key), matmul(flat_in.T, grad_value), matmul(attended.T, grad_layer_bf)], axis=1)
    weight_grads = jnp.concatenate([projection_grads, jnp.stack(conv_grads, axis=1)], axis=1)
    return features_grad, weight_grads
```

```python
import functools

import jax
import jax.numpy as jnp
from jax import lax
from jax.experimental import pallas as pl
from jax.experimental.pallas import tpu as pltpu
from jax.sharding import PartitionSpec as P

HEADS = 8
SECTOR = 64
TAPS = 27
MASKED = -1e30
GROUP = ("beam", "sweep")

NN = ((1,), (0,))
NT = ((1,), (1,))
TN = ((0,), (0,))

VMEM = pl.BlockSpec(memory_space=pltpu.VMEM)
SMEM = pl.BlockSpec(memory_space=pltpu.SMEM)
BF = jnp.bfloat16
F32 = jnp.float32


def dot(left, right, dims=NN):
    return lax.dot_general(left, right, (dims, ((), ())), preferred_element_type=F32)


def call(kernel, outs, in_specs, scratch=(), limit=40):
    return pl.pallas_call(
        kernel,
        out_shape=[jax.ShapeDtypeStruct(shape, dtype) for shape, dtype in outs],
        in_specs=in_specs,
        out_specs=[VMEM] * len(outs),
        scratch_shapes=list(scratch),
        compiler_params=pltpu.CompilerParams(vmem_limit_bytes=limit << 20),
    )


def slot_of(other, own):
    differ = other ^ own
    return (differ & 1) * 4 + (differ >> 1)


def group_index():
    return lax.axis_index("beam") * lax.axis_size("sweep") + lax.axis_index("sweep")


def prep_kernel(features_ref, cot_ref, features_out, cot_out):
    for source, target in ((features_ref, features_out), (cot_ref, cot_out)):
        wide = source[...].astype(F32)
        for b in range(wide.shape[1]):
            target[b] = wide[:, b, :].astype(BF)


def slices_kernel(even_ref, odd_ref, slices_out, first_out, last_out):
    me = group_index()
    _, beams, cols, channels = even_ref.shape
    width = channels // 8
    for out, col in ((first_out, 0), (last_out, cols - 1)):
        base = col // 16 * 16
        rows = []
        for ref in (even_ref, odd_ref):
            for block in range(4):
                for b in range(beams):
                    part = ref[block, b, base : base + 16, :].astype(F32)
                    rows.append(part[col - base : col - base + 1])
        out[...] = jnp.concatenate(rows, axis=0).astype(BF)
    channel = lax.broadcasted_iota(jnp.int32, (channels, 4 * width), 0) - width * me
    lane = lax.broadcasted_iota(jnp.int32, (channels, 4 * width), 1)
    total = [None] * 4
    for b in range(4):
        pick = jnp.where(channel + width * b == lane, 1.0, 0.0)
        pick = jnp.where((channel >= 0) & (channel < width), pick, 0.0).astype(BF)
        for s in range(4):
            slot = slot_of((b // beams) * 4 + s, me)
            odd = slot // 4
            block = lax.rem(slot, 4)
            value = jnp.where(odd == 1, odd_ref[block, b % beams], even_ref[block, b % beams])
            part = dot(value, pick)
            total[s] = part if total[s] is None else total[s] + part
    for s in range(4):
        slices_out[:, 4 * width * s : 4 * width * (s + 1)] = total[s].astype(BF)


def conv_kernel(even_ref, odd_ref, below_ref, above_ref, w_ref, w_out_ref, layer_out, layer_bf_out, attended_out,
                padded, edges, shifted):
    me = group_index()
    sweep = lax.axis_index("sweep")
    beam = lax.axis_index("beam")
    _, beams, cols, channels = even_ref.shape
    edges[0] = below_ref[...].astype(F32)
    edges[1] = above_ref[...].astype(F32)
    for j in range(3):
        other_sweep = sweep + (j - 1)
        sweep_ok = (other_sweep >= 0) & (other_sweep < 4)
        for m in range(beams + 2):
            other_beam = beam + (-1 if m == 0 else (1 if m == beams + 1 else 0))
            within = (m - 1) % beams
            ok = sweep_ok & (other_beam >= 0) & (other_beam < 2)
            keep = jnp.where(ok, 1.0, 0.0)
            other = jnp.where(ok, other_beam * 4 + other_sweep, me)
            slot = slot_of(other, me)
            odd = slot // 4
            block = lax.rem(slot, 4)
            value = jnp.where(odd == 1, odd_ref[block, within], even_ref[block, within])
            padded[j, m, 8 : 8 + cols, :] = value.astype(F32) * keep
            row = slot * beams + within
            padded[j, m, 7:8, :] = edges[0, pl.ds(row, 1), :] * keep
            padded[j, m, 8 + cols : 9 + cols, :] = edges[1, pl.ds(row, 1), :] * keep
    for i in (-1, 0, 1):
        for j in range(3):
            for m in range(beams + 2):
                shifted[i + 1, j, m * cols : (m + 1) * cols, :] = padded[j, m, 8 - i : 8 - i + cols, :].astype(BF)
    total = even_ref[0].reshape(beams * cols, channels).astype(F32)
    for i in (-1, 0, 1):
        for j in (-1, 0, 1):
            for k in (-1, 0, 1):
                rows = shifted[i + 1, 1 - j, (1 - k) * cols : (1 - k + beams) * cols, :]
                total = total + dot(rows, w_ref[9 * (i + 1) + 3 * (j + 1) + (k + 1)], NT)
    rounded = total.astype(BF)
    layer_out[...] = total.reshape(beams, cols, channels)
    layer_bf_out[...] = rounded.reshape(beams, cols, channels)
    attended_out[...] = dot(rounded, w_out_ref[...], NT).astype(BF).reshape(beams, cols, channels)


def allowed_row(mask_ref, count, cols):
    me = lax.axis_index("azim")
    block = lax.broadcasted_iota(jnp.int32, (1, count * cols), 1) // cols
    row = jnp.zeros((1, count * cols), jnp.int32)
    for ahead in range(count):
        row = jnp.where(block == ahead, mask_ref[me, lax.rem(me + ahead, count)], row)
    return row > 0


def by_head(rows):
    cols, channels = rows.shape
    head = lax.broadcasted_iota(jnp.int32, rows.shape, 1) // (channels // HEADS)
    wide = rows.astype(F32)
    return jnp.concatenate([jnp.where(head == h, wide, 0.0).astype(BF) for h in range(HEADS)], axis=0)


def own_head(stacked):
    cols = stacked.shape[0] // HEADS
    channels = stacked.shape[1]
    head = lax.broadcasted_iota(jnp.int32, (cols, channels), 1) // (channels // HEADS)
    total = jnp.zeros((cols, channels), F32)
    for h in range(HEADS):
        total = jnp.where(head == h, stacked[h * cols : (h + 1) * cols], total)
    return total


def weights_of(queries_by_head, keys, allowed):
    scale = (queries_by_head.shape[1] // HEADS) ** (-0.5)
    scores = jnp.where(allowed, dot(queries_by_head, keys, NT) * scale, MASKED)
    peak = jnp.max(scores, axis=-1, keepdims=True)
    logsum = peak + jnp.log(jnp.sum(jnp.exp(scores - peak), axis=-1, keepdims=True))
    return jnp.where(allowed, jnp.exp(scores - logsum), 0.0)


def forward_kernel(count, *refs):
    mask_ref = refs[0]
    feature_refs = refs[1 : 1 + count]
    w_query, w_key, w_value, w_out = refs[1 + count : 5 + count]
    all_out, query_out, key_out, value_out, attended_out, pieces_out = refs[5 + count :]
    beams, cols, channels = feature_refs[0].shape
    for ahead in range(count):
        all_out[:, ahead * cols : (ahead + 1) * cols, :] = feature_refs[ahead][...]
    own = feature_refs[0][...].reshape(beams * cols, channels)
    every = all_out[...].reshape(beams * count * cols, channels)
    query_out[...] = dot(own, w_query[...]).astype(BF).reshape(beams, cols, channels)
    key_out[...] = dot(every, w_key[...]).astype(BF).reshape(beams, count * cols, channels)
    value_out[...] = dot(every, w_value[...]).astype(BF).reshape(beams, count * cols, channels)
    allowed = allowed_row(mask_ref, count, cols)
    for b in range(beams):
        weights = weights_of(by_head(query_out[b]), key_out[b], allowed)
        attended_out[b] = own_head(dot(weights.astype(BF), value_out[b])).astype(BF)
    mixed = own.astype(F32) + dot(attended_out[...].reshape(beams * cols, channels), w_out[...])
    me = lax.axis_index("azim")
    width = channels // count
    for owner in range(count):
        part = [mixed[b * cols : (b + 1) * cols, owner * width : (owner + 1) * width] for b in range(beams)]
        pieces_out[lax.rem(owner + count - me, count)] = jnp.concatenate(part, axis=1).astype(BF)


def backward_kernel(count, mask_ref, all_ref, query_ref, key_ref, value_ref, attended_ref, grad_ref, layer_bf_ref,
                    layer_ref, w_query, w_key, w_value, base_out, send_out, keep_out, pass_out,
                    grad_query, grad_key, grad_value, sums):
    beams, cols, channels = query_ref.shape
    scale = (channels // HEADS) ** (-0.5)
    allowed = allowed_row(mask_ref, count, cols)
    for b in range(beams):
        queries = by_head(query_ref[b])
        keys = key_ref[b]
        weights = weights_of(queries, keys, allowed)
        grads = by_head(grad_ref[b])
        attended = jnp.concatenate([attended_ref[b].astype(F32)] * HEADS, axis=0)
        delta = jnp.sum(grads.astype(F32) * attended, axis=-1, keepdims=True)
        grad_score = (weights * (dot(grads, value_ref[b], NT) - delta)).astype(BF)
        grad_query[b] = (own_head(dot(grad_score, keys)) * scale).astype(BF)
        grad_key[b] = (dot(grad_score, queries, TN) * scale).astype(BF)
        grad_value[b] = dot(weights.astype(BF), grads, TN).astype(BF)
    own_rows = beams * cols
    all_rows = beams * count * cols
    query_flat = grad_query[...].reshape(own_rows, channels)
    key_flat = grad_key[...].reshape(all_rows, channels)
    value_flat = grad_value[...].reshape(all_rows, channels)
    own = dot(query_flat, w_query[...], NT).reshape(beams, cols, channels) + layer_ref[...]
    spread = dot(key_flat, w_key[...], NT) + dot(value_flat, w_value[...], NT)
    spread = spread.reshape(beams, count, cols, channels)
    base_out[...] = own + spread[:, 0]
    for ahead in range(1, count):
        send_out[ahead - 1] = spread[:, ahead].astype(BF)
    every = all_ref[...].reshape(all_rows, channels)
    mine = all_ref[:, :cols, :].reshape(own_rows, channels)
    width = channels // 8
    for index, (left, right) in enumerate(
        (
            (query_flat, mine),
            (key_flat, every),
            (value_flat, every),
            (layer_bf_ref[...].reshape(own_rows, channels), attended_ref[...].reshape(own_rows, channels)),
        )
    ):
        sums[index] = dot(left, right, TN).astype(BF).reshape(8, width, channels)
    me = group_index()
    for differ in range(8):
        target = pass_out if differ & 1 else keep_out
        for index in range(4):
            target[differ >> 1, index * width : (index + 1) * width, :] = sums[index, me ^ differ]


def pieces_kernel(count, keep_ref, come_ref, pieces_out):
    me = lax.axis_index("azim")
    total = keep_ref[...].astype(F32) + come_ref[...].astype(F32)
    rows, channels = total.shape
    width = channels // count
    half = rows // 2
    for owner in range(count):
        part = total[:, owner * width : (owner + 1) * width]
        pieces_out[lax.rem(owner + count - me, count)] = jnp.concatenate([part[:half], part[half:]], axis=1).astype(BF)


def last_kernel(count, *refs):
    even_ref, odd_ref, own_ref = refs[:3]
    packed_refs = refs[3 : 2 + count]
    own_piece = refs[2 + count]
    piece_refs = refs[3 + count : 2 + 2 * count]
    base_ref = refs[2 + 2 * count]
    come_refs = refs[3 + 2 * count : 2 + 3 * count]
    features_out, weights_out, layers, turned = refs[2 + 3 * count :]
    me = group_index()
    total = base_ref[...]
    for ref in come_refs:
        total = total + ref[...].astype(F32)
    features_out[...] = jnp.stack([total[b] for b in range(total.shape[0])], axis=1).astype(BF)
    piece = own_piece[0].astype(F32)
    for ref in piece_refs:
        piece = piece + ref[...].astype(F32)
    lanes = piece.shape[1] // 2
    width = piece.shape[0] // 2
    for index in range(4):
        weights_out[index] = piece[
            (index % 2) * width : (index % 2 + 1) * width, (index // 2) * lanes : (index // 2 + 1) * lanes
        ]
    rows = own_ref.shape[0]
    for s in range(4):
        for y in range(2):
            slot = slot_of(y * 4 + s, me)
            odd = slot // 4
            block = lax.rem(slot, 4)
            value = jnp.where(odd == 1, odd_ref[block], even_ref[block])
            layers[s, :, y * 2 * lanes : (y + 1) * 2 * lanes] = value.reshape(count * rows, 2 * lanes)
    span = own_ref.shape[1]
    cots = [own_ref[...]] + [ref[:, :span] for ref in packed_refs]
    wide = jnp.concatenate(cots, axis=0).astype(F32).T
    for i in (-1, 0, 1):
        moved = wide if i == 0 else pltpu.roll(wide, i % wide.shape[1], 1)
        turned[i + 1] = moved.astype(BF)
    per_sweep = span // 4
    for i in (-1, 0, 1):
        for j in (-1, 0, 1):
            found = None
            for s in range(4):
                if 0 <= s - j < 4:
                    part = dot(turned[i + 1, (s - j) * per_sweep : (s - j + 1) * per_sweep, :], layers[s])
                    found = part if found is None else found + part
            for k in (-1, 0, 1):
                tap = None
                for b in range(4):
                    if 0 <= b + k < 4:
                        part = found[b * width : (b + 1) * width, (b + k) * lanes : (b + k + 1) * lanes]
                        tap = part if tap is None else tap + part
                weights_out[4 + 9 * (i + 1) + 3 * (j + 1) + (k + 1)] = tap


def shift(value, ahead):
    count = lax.axis_size("azim")
    return lax.ppermute(value, "azim", [(i, (i + ahead) % count) for i in range(count)])


def swap(value, bits):
    return lax.ppermute(value, GROUP, [(i, i ^ bits) for i in range(8)])


def group_gather(value):
    even = jnp.stack([value, swap(value, 2), swap(value, 4), swap(value, 6)])
    return even, swap(even, 1)


def add(left, right):
    return (left.astype(F32) + right.astype(F32)).astype(BF)


def per_device(features, cotangent, w_query, w_key, w_value, w_out, w_conv, sector_mask):
    cols, sweeps, beams, channels = features.shape
    count = lax.axis_size("azim")
    assert sweeps == 1 and beams == 2 and cols == SECTOR
    assert lax.axis_size("beam") == 2 and lax.axis_size("sweep") == 4
    width = channels // 8
    lanes = channels // count
    block = (beams, cols, channels)
    whole = (beams, count * cols, channels)

    own_features, own_cot = call(prep_kernel, [(block, BF)] * 2, [VMEM] * 2)(
        features.reshape(cols, beams, channels), cotangent.reshape(cols, beams, channels)
    )
    come = [shift(own_features, ahead) for ahead in range(1, count)]
    all_features = [own_features] + come[::-1]
    even, odd = group_gather(own_cot)

    edge = (8 * beams, channels)
    slices, first, last = call(
        slices_kernel, [((cols, 16 * width), BF), (edge, BF), (edge, BF)], [VMEM] * 2
    )(even, odd)
    below = shift(last, 1)
    above = shift(first, count - 1)

    every, queries, keys, values, attended, pieces = call(
        functools.partial(forward_kernel, count),
        [(whole, BF), (block, BF), (whole, BF), (whole, BF), (block, BF), ((count, cols, beams * lanes), BF)],
        [SMEM] + [VMEM] * (count + 4),
    )(sector_mask, *all_features, w_query, w_key, w_value, w_out)

    span = 16 * width
    packed = [shift(jnp.concatenate([slices, pieces[ahead]], axis=1), ahead) for ahead in range(1, count)][::-1]
    layer_block = jnp.stack([pieces[0]] + [part[:, span:] for part in packed])
    even_layers, odd_layers = group_gather(layer_block)

    grad_layer, grad_layer_bf, grad_attended = call(
        conv_kernel,
        [(block, F32), (block, BF), (block, BF)],
        [VMEM] * 6,
        scratch=[
            pltpu.VMEM((3, beams + 2, cols + 16, channels), F32),
            pltpu.VMEM((2,) + edge, F32),
            pltpu.VMEM((3, 3, (beams + 2) * cols, channels), BF),
        ],
    )(even, odd, below, above, w_conv.transpose(1, 0, 2), w_out)

    quarter = (4, 4 * width, channels)
    base, send, keep, give = call(
        functools.partial(backward_kernel, count),
        [(block, F32), ((count - 1,) + block, BF), (quarter, BF), (quarter, BF)],
        [SMEM] + [VMEM] * 11,
        scratch=[
            pltpu.VMEM(block, BF),
            pltpu.VMEM(whole, BF),
            pltpu.VMEM(whole, BF),
            pltpu.VMEM((4, 8, width, channels), BF),
        ],
    )(
        sector_mask, every, queries, keys, values, attended, grad_attended, grad_layer_bf, grad_layer,
        w_query, w_key, w_value,
    )
    come_grads = [shift(send[ahead - 1], ahead) for ahead in range(1, count)]

    sums = add(keep, swap(give, 1)).reshape(2, 2, 4 * width, channels)
    sums = add(sums[:, 0], swap(sums[:, 1], 2))
    sum_pieces = call(
        functools.partial(pieces_kernel, count), [((count, 2 * width, 2 * lanes), BF)], [VMEM] * 2
    )(sums[0], swap(sums[1], 4))[0]
    come_pieces = [shift(sum_pieces[ahead], ahead) for ahead in range(1, count)]

    features_grad, weight_grads = call(
        functools.partial(last_kernel, count),
        [((cols, beams, channels), BF), ((4 + TAPS, width, lanes), F32)],
        [VMEM] * (2 + 3 * count),
        scratch=[
            pltpu.VMEM((4, count * cols, 4 * lanes), BF),
            pltpu.VMEM((3, span, count * cols), BF),
        ],
    )(even_layers, odd_layers, slices, *packed, sum_pieces, *come_pieces, base, *come_grads)
    return features_grad.reshape(features.shape), weight_grads.transpose(2, 0, 1)


def solution(mesh):
    token = P("azim", "sweep", "beam", None)
    in_specs = (token, token, P(), P(), P(), P(), P(), P())
    out_specs = (token, P("azim", None, ("beam", "sweep")))
    return jax.shard_map(per_device, mesh=mesh, in_specs=in_specs, out_specs=out_specs, check_vma=False)
```

```python
import functools

import jax
import jax.numpy as jnp
from jax import lax
from jax.experimental import pallas as pl
from jax.experimental.pallas import tpu as pltpu
from jax.sharding import PartitionSpec as P

HEADS = 8
SECTOR = 64
LANES = 128
TAPS = 27
MASKED = -1e30
GROUP = ("beam", "sweep")

NN = ((1,), (0,))
NT = ((1,), (1,))
TN = ((0,), (0,))

VMEM = pl.BlockSpec(memory_space=pltpu.VMEM)
HBM = pl.BlockSpec(memory_space=pltpu.HBM)
BF = jnp.bfloat16
F32 = jnp.float32


def dot(left, right, dims=NN):
    return lax.dot_general(left, right, (dims, ((), ())), preferred_element_type=F32)


def call(kernel, outs, in_specs, scratch=(), limit=40):
    return pl.pallas_call(
        kernel,
        out_shape=[jax.ShapeDtypeStruct(shape, dtype) for shape, dtype in outs],
        in_specs=in_specs,
        out_specs=[VMEM] * len(outs),
        scratch_shapes=list(scratch),
        compiler_params=pltpu.CompilerParams(vmem_limit_bytes=limit << 20),
    )


def slot_of(other, own):
    differ = other ^ own
    return (differ & 1) * 4 + (differ >> 1)


def group_index():
    return lax.axis_index("beam") * lax.axis_size("sweep") + lax.axis_index("sweep")


def prep_kernel(count, features_hbm, cot_hbm, mask_hbm, *refs):
    weights_hbm = refs[:4]
    features_out, cot_out, allowed_out = refs[4:7]
    weights_out = refs[7:11]
    features, cot, mask, sems = refs[11:]
    copies = [
        pltpu.make_async_copy(source, target, sems.at[index])
        for index, (source, target) in enumerate(
            zip((features_hbm, cot_hbm, mask_hbm) + weights_hbm, (features, cot, mask) + weights_out)
        )
    ]
    for copy in copies:
        copy.start()
    for copy, source, target in ((copies[0], features, features_out), (copies[1], cot, cot_out)):
        copy.wait()
        wide = source[...].astype(F32)
        for b in range(wide.shape[1]):
            target[b] = wide[:, b, :].astype(BF)
    copies[2].wait()
    me = lax.axis_index("azim")
    square = mask[...].astype(F32)
    row = lax.broadcasted_iota(jnp.int32, square.shape, 0)
    own = jnp.sum(jnp.where(row == me, square, 0.0), axis=0, keepdims=True)
    keys = allowed_out.shape[1]
    sector = lax.broadcasted_iota(jnp.int32, (count, keys), 0)
    block = lax.broadcasted_iota(jnp.int32, (count, keys), 1) // SECTOR
    spread = jnp.where(sector == lax.rem(block + me, count), 1.0, 0.0).astype(BF)
    allowed_out[...] = dot(jnp.broadcast_to(own, (8, count)).astype(BF), spread)
    for copy in copies[3:]:
        copy.wait()


def slices_kernel(even_ref, odd_ref, slices_out, first_out, last_out):
    me = group_index()
    _, beams, cols, channels = even_ref.shape
    width = channels // 8
    for out, col in ((first_out, 0), (last_out, cols - 1)):
        base = col // 16 * 16
        rows = []
        for ref in (even_ref, odd_ref):
            for block in range(4):
                for b in range(beams):
                    part = ref[block, b, base : base + 16, :].astype(F32)
                    rows.append(part[col - base : col - base + 1])
        edge = jnp.concatenate(rows, axis=0).astype(BF)
        count = edge.shape[0]
        for half in range(out.shape[0] // count):
            out[half * count : (half + 1) * count] = edge[:, half * LANES : (half + 1) * LANES]
    channel = lax.broadcasted_iota(jnp.int32, (channels, 4 * width), 0) - width * me
    lane = lax.broadcasted_iota(jnp.int32, (channels, 4 * width), 1)
    total = [None] * 4
    for b in range(4):
        pick = jnp.where(channel + width * b == lane, 1.0, 0.0)
        pick = jnp.where((channel >= 0) & (channel < width), pick, 0.0).astype(BF)
        for s in range(4):
            slot = slot_of((b // beams) * 4 + s, me)
            odd = slot // 4
            block = lax.rem(slot, 4)
            value = jnp.where(odd == 1, odd_ref[block, b % beams], even_ref[block, b % beams])
            part = dot(value, pick)
            total[s] = part if total[s] is None else total[s] + part
    for s in range(4):
        slices_out[cols * s : cols * (s + 1), :] = total[s].astype(BF)


def conv_kernel(even_ref, odd_ref, below_ref, above_ref, w_ref, w_out_ref, layer_out, layer_bf_out, attended_out,
                padded, edges, shifted):
    me = group_index()
    sweep = lax.axis_index("sweep")
    beam = lax.axis_index("beam")
    _, beams, cols, channels = even_ref.shape
    count = 8 * beams
    start = below_ref.shape[0] - count * (channels // LANES)
    for index, ref in enumerate((below_ref, above_ref)):
        for half in range(channels // LANES):
            edges[index, :, half * LANES : (half + 1) * LANES] = ref[
                start + half * count : start + (half + 1) * count, :
            ].astype(F32)
    for j in range(3):
        other_sweep = sweep + (j - 1)
        sweep_ok = (other_sweep >= 0) & (other_sweep < 4)
        for m in range(beams + 2):
            other_beam = beam + (-1 if m == 0 else (1 if m == beams + 1 else 0))
            within = (m - 1) % beams
            ok = sweep_ok & (other_beam >= 0) & (other_beam < 2)
            keep = jnp.where(ok, 1.0, 0.0)
            other = jnp.where(ok, other_beam * 4 + other_sweep, me)
            slot = slot_of(other, me)
            odd = slot // 4
            block = lax.rem(slot, 4)
            value = jnp.where(odd == 1, odd_ref[block, within], even_ref[block, within])
            padded[j, m, 8 : 8 + cols, :] = value.astype(F32) * keep
            row = slot * beams + within
            padded[j, m, 7:8, :] = edges[0, pl.ds(row, 1), :] * keep
            padded[j, m, 8 + cols : 9 + cols, :] = edges[1, pl.ds(row, 1), :] * keep
    for i in (-1, 0, 1):
        for j in range(3):
            for m in range(beams + 2):
                shifted[i + 1, j, m * cols : (m + 1) * cols, :] = padded[j, m, 8 - i : 8 - i + cols, :].astype(BF)
    total = even_ref[0].reshape(beams * cols, channels).astype(F32)
    for i in (-1, 0, 1):
        for j in (-1, 0, 1):
            for k in (-1, 0, 1):
                rows = shifted[i + 1, 1 - j, (1 - k) * cols : (1 - k + beams) * cols, :]
                total = total + dot(rows, w_ref[9 * (i + 1) + 3 * (j + 1) + (k + 1)], NT)
    rounded = total.astype(BF)
    layer_out[...] = total.reshape(beams, cols, channels)
    layer_bf_out[...] = rounded.reshape(beams, cols, channels)
    attended_out[...] = dot(rounded, w_out_ref[...], NT).astype(BF).reshape(beams, cols, channels)


def by_head(rows):
    cols, channels = rows.shape
    head = lax.broadcasted_iota(jnp.int32, rows.shape, 1) // (channels // HEADS)
    wide = rows.astype(F32)
    return jnp.concatenate([jnp.where(head == h, wide, 0.0).astype(BF) for h in range(HEADS)], axis=0)


def own_head(stacked):
    cols = stacked.shape[0] // HEADS
    channels = stacked.shape[1]
    head = lax.broadcasted_iota(jnp.int32, (cols, channels), 1) // (channels // HEADS)
    total = jnp.zeros((cols, channels), F32)
    for h in range(HEADS):
        total = jnp.where(head == h, stacked[h * cols : (h + 1) * cols], total)
    return total


def weights_of(queries_by_head, keys, allowed):
    scale = (queries_by_head.shape[1] // HEADS) ** (-0.5)
    scores = jnp.where(allowed, dot(queries_by_head, keys, NT) * scale, MASKED)
    peak = jnp.max(scores, axis=-1, keepdims=True)
    logsum = peak + jnp.log(jnp.sum(jnp.exp(scores - peak), axis=-1, keepdims=True))
    return jnp.where(allowed, jnp.exp(scores - logsum), 0.0)


def forward_kernel(count, *refs):
    allowed_ref = refs[0]
    feature_refs = refs[1 : 1 + count]
    w_query, w_key, w_value, w_out, w_conv_hbm = refs[1 + count : 6 + count]
    all_out, query_out, key_out, value_out, attended_out, pieces_out, w_conv_out, sem = refs[6 + count :]
    copy = pltpu.make_async_copy(w_conv_hbm, w_conv_out, sem)
    copy.start()
    beams, cols, channels = feature_refs[0].shape
    for ahead in range(count):
        all_out[:, ahead * cols : (ahead + 1) * cols, :] = feature_refs[ahead][...]
    own = feature_refs[0][...].reshape(beams * cols, channels)
    every = all_out[...].reshape(beams * count * cols, channels)
    query_out[...] = dot(own, w_query[...]).astype(BF).reshape(beams, cols, channels)
    key_out[...] = dot(every, w_key[...]).astype(BF).reshape(beams, count * cols, channels)
    value_out[...] = dot(every, w_value[...]).astype(BF).reshape(beams, count * cols, channels)
    allowed = allowed_ref[0:1, :] > 0.5
    for b in range(beams):
        weights = weights_of(by_head(query_out[b]), key_out[b], allowed)
        attended_out[b] = own_head(dot(weights.astype(BF), value_out[b])).astype(BF)
    mixed = own.astype(F32) + dot(attended_out[...].reshape(beams * cols, channels), w_out[...])
    me = lax.axis_index("azim")
    width = channels // count
    for owner in range(count):
        part = [mixed[b * cols : (b + 1) * cols, owner * width : (owner + 1) * width] for b in range(beams)]
        spare = pieces_out.shape[2] - beams * width
        if spare:
            part.append(jnp.zeros((cols, spare), F32))
        pieces_out[lax.rem(owner + count - me, count)] = jnp.concatenate(part, axis=1).astype(BF)
    copy.wait()


def backward_kernel(count, allowed_ref, all_ref, query_ref, key_ref, value_ref, attended_ref, grad_ref, layer_bf_ref,
                    layer_ref, w_query, w_key, w_value, base_out, send_out, keep_out, pass_out,
                    grad_query, grad_key, grad_value, sums):
    beams, cols, channels = query_ref.shape
    scale = (channels // HEADS) ** (-0.5)
    allowed = allowed_ref[0:1, :] > 0.5
    for b in range(beams):
        queries = by_head(query_ref[b])
        keys = key_ref[b]
        weights = weights_of(queries, keys, allowed)
        grads = by_head(grad_ref[b])
        attended = jnp.concatenate([attended_ref[b].astype(F32)] * HEADS, axis=0)
        delta = jnp.sum(grads.astype(F32) * attended, axis=-1, keepdims=True)
        grad_score = (weights * (dot(grads, value_ref[b], NT) - delta)).astype(BF)
        grad_query[b] = (own_head(dot(grad_score, keys)) * scale).astype(BF)
        grad_key[b] = (dot(grad_score, queries, TN) * scale).astype(BF)
        grad_value[b] = dot(weights.astype(BF), grads, TN).astype(BF)
    own_rows = beams * cols
    all_rows = beams * count * cols
    query_flat = grad_query[...].reshape(own_rows, channels)
    key_flat = grad_key[...].reshape(all_rows, channels)
    value_flat = grad_value[...].reshape(all_rows, channels)
    own = dot(query_flat, w_query[...], NT).reshape(beams, cols, channels) + layer_ref[...]
    spread = dot(key_flat, w_key[...], NT) + dot(value_flat, w_value[...], NT)
    spread = spread.reshape(beams, count, cols, channels)
    base_out[...] = own + spread[:, 0]
    for ahead in range(1, count):
        send_out[ahead - 1] = spread[:, ahead].astype(BF)
    every = all_ref[...].reshape(all_rows, channels)
    mine = all_ref[:, :cols, :].reshape(own_rows, channels)
    width = channels // 8
    for index, (left, right) in enumerate(
        (
            (query_flat, mine),
            (key_flat, every),
            (value_flat, every),
            (layer_bf_ref[...].reshape(own_rows, channels), attended_ref[...].reshape(own_rows, channels)),
        )
    ):
        sums[index] = dot(left, right, TN).astype(BF).reshape(8, width, channels)
    me = group_index()
    for differ in range(8):
        target = pass_out if differ & 1 else keep_out
        for index in range(4):
            target[differ >> 1, index * width : (index + 1) * width, :] = sums[index, me ^ differ]


def pieces_kernel(count, keep_ref, come_ref, pieces_out):
    me = lax.axis_index("azim")
    total = keep_ref[...].astype(F32) + come_ref[...].astype(F32)
    rows, channels = total.shape
    width = channels // count
    half = rows // 2
    for owner in range(count):
        part = total[:, owner * width : (owner + 1) * width]
        pieces_out[lax.rem(owner + count - me, count)] = jnp.concatenate([part[:half], part[half:]], axis=1).astype(BF)


def last_kernel(count, *refs):
    even_ref, odd_ref, own_ref = refs[:3]
    packed_refs = refs[3 : 2 + count]
    own_piece = refs[2 + count]
    piece_refs = refs[3 + count : 2 + 2 * count]
    base_ref = refs[2 + 2 * count]
    come_refs = refs[3 + 2 * count : 2 + 3 * count]
    features_out, weights_out, layers, turned = refs[2 + 3 * count :]
    me = group_index()
    total = base_ref[...]
    for ref in come_refs:
        total = total + ref[...].astype(F32)
    features_out[...] = jnp.stack([total[b] for b in range(total.shape[0])], axis=1).astype(BF)
    piece = own_piece[0].astype(F32)
    for ref in piece_refs:
        piece = piece + ref[...].astype(F32)
    lanes = piece.shape[1] // 2
    width = piece.shape[0] // 2
    for index in range(4):
        weights_out[index] = piece[
            (index % 2) * width : (index % 2 + 1) * width, (index // 2) * lanes : (index // 2 + 1) * lanes
        ]
    per_sweep, rows = own_ref.shape[1], own_ref.shape[0] // 4
    for s in range(4):
        for y in range(2):
            slot = slot_of(y * 4 + s, me)
            odd = slot // 4
            block = lax.rem(slot, 4)
            value = jnp.where(odd == 1, odd_ref[block], even_ref[block])
            layers[s, :, y * 2 * lanes : (y + 1) * 2 * lanes] = value.reshape(count * rows, -1)[:, : 2 * lanes]
    for s in range(4):
        cots = [ref[s * rows : (s + 1) * rows, :] for ref in (own_ref,) + tuple(packed_refs)]
        wide = jnp.concatenate(cots, axis=0).astype(F32).T
        for i in (-1, 0, 1):
            moved = wide if i == 0 else pltpu.roll(wide, i % wide.shape[1], 1)
            turned[i + 1, s * per_sweep : (s + 1) * per_sweep, :] = moved.astype(BF)
    for i in (-1, 0, 1):
        for j in (-1, 0, 1):
            found = None
            for s in range(4):
                if 0 <= s - j < 4:
                    part = dot(turned[i + 1, (s - j) * per_sweep : (s - j + 1) * per_sweep, :], layers[s])
                    found = part if found is None else found + part
            for k in (-1, 0, 1):
                tap = None
                for b in range(4):
                    if 0 <= b + k < 4:
                        part = found[b * width : (b + 1) * width, (b + k) * lanes : (b + k + 1) * lanes]
                        tap = part if tap is None else tap + part
                weights_out[4 + 9 * (i + 1) + 3 * (j + 1) + (k + 1)] = tap


def in_hbm(value):
    return pltpu.with_memory_space_constraint(value, pltpu.HBM)


def shift(value, ahead):
    count = lax.axis_size("azim")
    return lax.ppermute(value, "azim", [(i, (i + ahead) % count) for i in range(count)])


def swap(value, bits):
    return lax.ppermute(value, GROUP, [(i, i ^ bits) for i in range(8)])


def group_gather(value):
    even = jnp.stack([value, swap(value, 2), swap(value, 4), swap(value, 6)])
    return even, swap(even, 1)


def add(left, right):
    return (left.astype(F32) + right.astype(F32)).astype(BF)


def per_device(features, cotangent, w_query, w_key, w_value, w_out, w_conv, sector_mask):
    cols, sweeps, beams, channels = features.shape
    count = lax.axis_size("azim")
    assert sweeps == 1 and beams == 2 and cols == SECTOR
    assert lax.axis_size("beam") == 2 and lax.axis_size("sweep") == 4
    width = channels // 8
    lanes = channels // count
    block = (beams, cols, channels)
    whole = (beams, count * cols, channels)

    token = (cols, beams, channels)
    square = (channels, channels)
    own_features, own_cot, allowed, w_query, w_key, w_value, w_out = call(
        functools.partial(prep_kernel, count),
        [(block, BF), (block, BF), ((8, count * cols), F32)] + [(square, BF)] * 4,
        [HBM] * 7,
        scratch=[
            pltpu.VMEM(token, BF),
            pltpu.VMEM(token, BF),
            pltpu.VMEM(sector_mask.shape, jnp.int32),
            pltpu.SemaphoreType.DMA((7,)),
        ],
    )(*map(in_hbm, (features.reshape(token), cotangent.reshape(token), sector_mask, w_query, w_key, w_value, w_out)))
    come = [shift(own_features, ahead) for ahead in range(1, count)]
    all_features = [own_features] + come[::-1]
    even, odd = group_gather(own_cot)

    spread = (4 * cols, 4 * width)
    edge = (8 * beams, channels)
    edge_rows = (8 * beams * channels // LANES, LANES)
    slices, first, last = call(
        slices_kernel, [(spread, BF), (edge_rows, BF), (edge_rows, BF)], [VMEM] * 2
    )(even, odd)

    pieces_shape = (count, cols, max(LANES, beams * lanes))
    every, queries, keys, values, attended, pieces, w_conv = call(
        functools.partial(forward_kernel, count),
        [(whole, BF), (block, BF), (whole, BF), (whole, BF), (block, BF), (pieces_shape, BF),
         ((TAPS,) + square, BF)],
        [VMEM] * (count + 5) + [HBM],
        scratch=[pltpu.SemaphoreType.DMA],
    )(allowed, *all_features, w_query, w_key, w_value, w_out, in_hbm(w_conv.transpose(1, 0, 2)))

    packed = []
    for ahead in range(1, count):
        parts = [slices, pieces[ahead]]
        if ahead == 1:
            parts.append(last)
        if ahead == count - 1:
            parts.append(first)
        packed.append(shift(jnp.concatenate(parts, axis=0), ahead))
    packed = packed[::-1]
    below, above = packed[-1], packed[0]
    start = 4 * cols
    layer_block = jnp.stack([pieces[0]] + [part[start : start + cols] for part in packed])
    even_layers, odd_layers = group_gather(layer_block)

    grad_layer, grad_layer_bf, grad_attended = call(
        conv_kernel,
        [(block, F32), (block, BF), (block, BF)],
        [VMEM] * 6,
        scratch=[
            pltpu.VMEM((3, beams + 2, cols + 16, channels), F32),
            pltpu.VMEM((2,) + edge, F32),
            pltpu.VMEM((3, 3, (beams + 2) * cols, channels), BF),
        ],
    )(even, odd, below, above, w_conv, w_out)

    quarter = (4, 4 * width, channels)
    base, send, keep, give = call(
        functools.partial(backward_kernel, count),
        [(block, F32), ((count - 1,) + block, BF), (quarter, BF), (quarter, BF)],
        [VMEM] * 12,
        scratch=[
            pltpu.VMEM(block, BF),
            pltpu.VMEM(whole, BF),
            pltpu.VMEM(whole, BF),
            pltpu.VMEM((4, 8, width, channels), BF),
        ],
    )(
        allowed, every, queries, keys, values, attended, grad_attended, grad_layer_bf, grad_layer,
        w_query, w_key, w_value,
    )
    come_grads = [shift(send[ahead - 1], ahead) for ahead in range(1, count)]

    sums = add(keep, swap(give, 1)).reshape(2, 2, 4 * width, channels)
    sums = add(sums[:, 0], swap(sums[:, 1], 2))
    sum_pieces = call(
        functools.partial(pieces_kernel, count), [((count, 2 * width, 2 * lanes), BF)], [VMEM] * 2
    )(sums[0], swap(sums[1], 4))[0]
    come_pieces = [shift(sum_pieces[ahead], ahead) for ahead in range(1, count)]

    features_grad, weight_grads = call(
        functools.partial(last_kernel, count),
        [((cols, beams, channels), BF), ((4 + TAPS, width, lanes), F32)],
        [VMEM] * (2 + 3 * count),
        scratch=[
            pltpu.VMEM((4, count * cols, 4 * lanes), BF),
            pltpu.VMEM((3, 16 * width, count * cols), BF),
        ],
    )(even_layers, odd_layers, slices, *packed, sum_pieces, *come_pieces, base, *come_grads)
    return features_grad.reshape(features.shape), weight_grads.transpose(2, 0, 1)


def solution(mesh):
    token = P("azim", "sweep", "beam", None)
    in_specs = (token, token, P(), P(), P(), P(), P(), P())
    out_specs = (token, P("azim", None, ("beam", "sweep")))
    return jax.shard_map(per_device, mesh=mesh, in_specs=in_specs, out_specs=out_specs, check_vma=False)
```

```python
import functools

import jax
import jax.numpy as jnp
from jax import lax
from jax.experimental import pallas as pl
from jax.experimental.pallas import tpu as pltpu
from jax.sharding import PartitionSpec as P

HEADS = 8
SECTOR = 64
LANES = 128
TAPS = 27
MASKED = -1e30
GROUP = ("beam", "sweep")

NN = ((1,), (0,))
NT = ((1,), (1,))
TN = ((0,), (0,))

VMEM = pl.BlockSpec(memory_space=pltpu.VMEM)
HBM = pl.BlockSpec(memory_space=pltpu.HBM)
BF = jnp.bfloat16
F32 = jnp.float32


def dot(left, right, dims=NN):
    return lax.dot_general(left, right, (dims, ((), ())), preferred_element_type=F32)


def call(kernel, outs, in_specs, scratch=(), limit=40):
    return pl.pallas_call(
        kernel,
        out_shape=[jax.ShapeDtypeStruct(shape, dtype) for shape, dtype in outs],
        in_specs=in_specs,
        out_specs=[VMEM] * len(outs),
        scratch_shapes=list(scratch),
        compiler_params=pltpu.CompilerParams(vmem_limit_bytes=limit << 20),
    )


def slot_of(other, own):
    differ = other ^ own
    return (differ & 1) * 4 + (differ >> 1)


def group_index():
    return lax.axis_index("beam") * lax.axis_size("sweep") + lax.axis_index("sweep")


def prep_kernel(count, features_hbm, cot_hbm, mask_hbm, *refs):
    weights_hbm = refs[:4]
    features_out, cot_out, allowed_out = refs[4:7]
    weights_out = refs[7:11]
    features, cot, mask, sems = refs[11:]
    copies = [
        pltpu.make_async_copy(source, target, sems.at[index])
        for index, (source, target) in enumerate(
            zip((features_hbm, cot_hbm, mask_hbm) + weights_hbm, (features, cot, mask) + weights_out)
        )
    ]
    for copy in copies:
        copy.start()
    for copy, source, target in ((copies[0], features, features_out), (copies[1], cot, cot_out)):
        copy.wait()
        wide = source[...].astype(F32)
        for b in range(wide.shape[1]):
            target[b] = wide[:, b, :].astype(BF)
    copies[2].wait()
    me = lax.axis_index("azim")
    square = mask[...].astype(F32)
    row = lax.broadcasted_iota(jnp.int32, square.shape, 0)
    own = jnp.sum(jnp.where(row == me, square, 0.0), axis=0, keepdims=True)
    keys = allowed_out.shape[1]
    sector = lax.broadcasted_iota(jnp.int32, (count, keys), 0)
    block = lax.broadcasted_iota(jnp.int32, (count, keys), 1) // SECTOR
    spread = jnp.where(sector == block ^ me, 1.0, 0.0).astype(BF)
    allowed_out[...] = dot(jnp.broadcast_to(own, (8, count)).astype(BF), spread)
    for copy in copies[3:]:
        copy.wait()


def slices_kernel(even_ref, odd_ref, slices_out, edges_out):
    me = group_index()
    _, beams, cols, channels = even_ref.shape
    width = channels // 8
    for side, col in enumerate((0, cols - 1)):
        base = col // 16 * 16
        rows = []
        for ref in (even_ref, odd_ref):
            for block in range(4):
                for b in range(beams):
                    part = ref[block, b, base : base + 16, :].astype(F32)
                    rows.append(part[col - base : col - base + 1])
        edges_out[side] = jnp.concatenate(rows, axis=0).astype(BF)
    channel = lax.broadcasted_iota(jnp.int32, (channels, 4 * width), 0) - width * me
    lane = lax.broadcasted_iota(jnp.int32, (channels, 4 * width), 1)
    total = [None] * 4
    for b in range(4):
        pick = jnp.where(channel + width * b == lane, 1.0, 0.0)
        pick = jnp.where((channel >= 0) & (channel < width), pick, 0.0).astype(BF)
        for s in range(4):
            slot = slot_of((b // beams) * 4 + s, me)
            odd = slot // 4
            block = lax.rem(slot, 4)
            value = jnp.where(odd == 1, odd_ref[block, b % beams], even_ref[block, b % beams])
            part = dot(value, pick)
            total[s] = part if total[s] is None else total[s] + part
    for s in range(4):
        slices_out[cols * s : cols * (s + 1), :] = total[s].astype(BF)


def neighbour_distances(count):
    return [distance for distance in range(1, count) if distance & (distance + 1) == 0]


def conv_kernel(count, even_ref, odd_ref, *refs):
    distances = neighbour_distances(count)
    edge_refs = refs[: len(distances)]
    w_ref, w_out_ref, layer_out, layer_bf_out, attended_out, padded, edges, shifted = refs[len(distances) :]
    me = group_index()
    column = lax.axis_index("azim")
    sweep = lax.axis_index("sweep")
    beam = lax.axis_index("beam")
    _, beams, cols, channels = even_ref.shape
    for index, step in enumerate((count - 1, 1)):
        partner = lax.rem(column + step, count) ^ column
        total = None
        for distance, ref in zip(distances, edge_refs):
            part = ref[1 - index].astype(F32) * jnp.where(partner == distance, 1.0, 0.0)
            total = part if total is None else total + part
        edges[index] = total
    for j in range(3):
        other_sweep = sweep + (j - 1)
        sweep_ok = (other_sweep >= 0) & (other_sweep < 4)
        for m in range(beams + 2):
            other_beam = beam + (-1 if m == 0 else (1 if m == beams + 1 else 0))
            within = (m - 1) % beams
            ok = sweep_ok & (other_beam >= 0) & (other_beam < 2)
            keep = jnp.where(ok, 1.0, 0.0)
            other = jnp.where(ok, other_beam * 4 + other_sweep, me)
            slot = slot_of(other, me)
            odd = slot // 4
            block = lax.rem(slot, 4)
            value = jnp.where(odd == 1, odd_ref[block, within], even_ref[block, within])
            padded[j, m, 8 : 8 + cols, :] = value.astype(F32) * keep
            row = slot * beams + within
            padded[j, m, 7:8, :] = edges[0, pl.ds(row, 1), :] * keep
            padded[j, m, 8 + cols : 9 + cols, :] = edges[1, pl.ds(row, 1), :] * keep
    for i in (-1, 0, 1):
        for j in range(3):
            for m in range(beams + 2):
                shifted[i + 1, j, m * cols : (m + 1) * cols, :] = padded[j, m, 8 - i : 8 - i + cols, :].astype(BF)
    total = even_ref[0].reshape(beams * cols, channels).astype(F32)
    for i in (-1, 0, 1):
        for j in (-1, 0, 1):
            for k in (-1, 0, 1):
                rows = shifted[i + 1, 1 - j, (1 - k) * cols : (1 - k + beams) * cols, :]
                total = total + dot(rows, w_ref[9 * (i + 1) + 3 * (j + 1) + (k + 1)], NT)
    rounded = total.astype(BF)
    layer_out[...] = total.reshape(beams, cols, channels)
    layer_bf_out[...] = rounded.reshape(beams, cols, channels)
    attended_out[...] = dot(rounded, w_out_ref[...], NT).astype(BF).reshape(beams, cols, channels)


def by_head(rows):
    cols, channels = rows.shape
    head = lax.broadcasted_iota(jnp.int32, rows.shape, 1) // (channels // HEADS)
    wide = rows.astype(F32)
    return jnp.concatenate([jnp.where(head == h, wide, 0.0).astype(BF) for h in range(HEADS)], axis=0)


def own_head(stacked):
    cols = stacked.shape[0] // HEADS
    channels = stacked.shape[1]
    head = lax.broadcasted_iota(jnp.int32, (cols, channels), 1) // (channels // HEADS)
    total = jnp.zeros((cols, channels), F32)
    for h in range(HEADS):
        total = jnp.where(head == h, stacked[h * cols : (h + 1) * cols], total)
    return total


def weights_of(queries_by_head, keys, allowed):
    scale = (queries_by_head.shape[1] // HEADS) ** (-0.5)
    scores = jnp.where(allowed, dot(queries_by_head, keys, NT) * scale, MASKED)
    peak = jnp.max(scores, axis=-1, keepdims=True)
    logsum = peak + jnp.log(jnp.sum(jnp.exp(scores - peak), axis=-1, keepdims=True))
    return jnp.where(allowed, jnp.exp(scores - logsum), 0.0)


def forward_kernel(count, *refs):
    allowed_ref = refs[0]
    feature_refs = refs[1 : 1 + count]
    w_query, w_key, w_value, w_out, w_conv_hbm = refs[1 + count : 6 + count]
    all_out, query_out, key_out, value_out, attended_out, pieces_out, w_conv_out, sem = refs[6 + count :]
    copy = pltpu.make_async_copy(w_conv_hbm, w_conv_out, sem)
    copy.start()
    beams, cols, channels = feature_refs[0].shape
    for ahead in range(count):
        all_out[:, ahead * cols : (ahead + 1) * cols, :] = feature_refs[ahead][...]
    own = feature_refs[0][...].reshape(beams * cols, channels)
    every = all_out[...].reshape(beams * count * cols, channels)
    query_out[...] = dot(own, w_query[...]).astype(BF).reshape(beams, cols, channels)
    key_out[...] = dot(every, w_key[...]).astype(BF).reshape(beams, count * cols, channels)
    value_out[...] = dot(every, w_value[...]).astype(BF).reshape(beams, count * cols, channels)
    allowed = allowed_ref[0:1, :] > 0.5
    for b in range(beams):
        weights = weights_of(by_head(query_out[b]), key_out[b], allowed)
        attended_out[b] = own_head(dot(weights.astype(BF), value_out[b])).astype(BF)
    mixed = own.astype(F32) + dot(attended_out[...].reshape(beams * cols, channels), w_out[...])
    me = lax.axis_index("azim")
    width = channels // count
    for owner in range(count):
        part = [mixed[b * cols : (b + 1) * cols, owner * width : (owner + 1) * width] for b in range(beams)]
        spare = pieces_out.shape[2] - beams * width
        if spare:
            part.append(jnp.zeros((cols, spare), F32))
        pieces_out[owner ^ me] = jnp.concatenate(part, axis=1).astype(BF)
    copy.wait()


def backward_kernel(count, allowed_ref, all_ref, query_ref, key_ref, value_ref, attended_ref, grad_ref, layer_bf_ref,
                    layer_ref, w_query, w_key, w_value, base_out, send_out, keep_out, pass_out,
                    grad_query, grad_key, grad_value, sums):
    beams, cols, channels = query_ref.shape
    scale = (channels // HEADS) ** (-0.5)
    allowed = allowed_ref[0:1, :] > 0.5
    for b in range(beams):
        queries = by_head(query_ref[b])
        keys = key_ref[b]
        weights = weights_of(queries, keys, allowed)
        grads = by_head(grad_ref[b])
        attended = jnp.concatenate([attended_ref[b].astype(F32)] * HEADS, axis=0)
        delta = jnp.sum(grads.astype(F32) * attended, axis=-1, keepdims=True)
        grad_score = (weights * (dot(grads, value_ref[b], NT) - delta)).astype(BF)
        grad_query[b] = (own_head(dot(grad_score, keys)) * scale).astype(BF)
        grad_key[b] = (dot(grad_score, queries, TN) * scale).astype(BF)
        grad_value[b] = dot(weights.astype(BF), grads, TN).astype(BF)
    own_rows = beams * cols
    all_rows = beams * count * cols
    query_flat = grad_query[...].reshape(own_rows, channels)
    key_flat = grad_key[...].reshape(all_rows, channels)
    value_flat = grad_value[...].reshape(all_rows, channels)
    own = dot(query_flat, w_query[...], NT).reshape(beams, cols, channels) + layer_ref[...]
    spread = dot(key_flat, w_key[...], NT) + dot(value_flat, w_value[...], NT)
    spread = spread.reshape(beams, count, cols, channels)
    base_out[...] = own + spread[:, 0]
    for ahead in range(1, count):
        part = spread[:, ahead].astype(BF).reshape(beams * cols, channels)
        for half in range(channels // LANES):
            send_out[ahead - 1, half * beams * cols : (half + 1) * beams * cols, :] = part[
                :, half * LANES : (half + 1) * LANES
            ]
    every = all_ref[...].reshape(all_rows, channels)
    mine = all_ref[:, :cols, :].reshape(own_rows, channels)
    width = channels // 8
    for index, (left, right) in enumerate(
        (
            (query_flat, mine),
            (key_flat, every),
            (value_flat, every),
            (layer_bf_ref[...].reshape(own_rows, channels), attended_ref[...].reshape(own_rows, channels)),
        )
    ):
        sums[index] = dot(left, right, TN).astype(BF).reshape(8, width, channels)
    me = group_index()
    for differ in range(8):
        target = pass_out if differ & 1 else keep_out
        for index in range(4):
            part = sums[index, me ^ differ]
            for half in range(channels // LANES):
                row = (half * 4 + index) * width
                target[differ >> 1, row : row + width, :] = part[:, half * LANES : (half + 1) * LANES]


def pieces_kernel(count, keep_ref, *refs):
    pieces_out = refs[-1]
    me = lax.axis_index("azim")
    rows = keep_ref.shape[0]
    total = keep_ref[...].astype(F32)
    for ref in refs[:-1]:
        total = total + ref[ref.shape[0] - rows :, :].astype(F32)
    halves = 2
    rows = rows // halves
    total = jnp.concatenate([total[half * rows : (half + 1) * rows] for half in range(halves)], axis=1)
    width = total.shape[1] // count
    half = rows // 2
    for owner in range(count):
        part = total[:, owner * width : (owner + 1) * width]
        part = [part[:half], part[half:]]
        spare = pieces_out.shape[2] - 2 * width
        if spare:
            part.append(jnp.zeros((half, spare), F32))
        pieces_out[owner ^ me] = jnp.concatenate(part, axis=1).astype(BF)


def taps_kernel(count, even_ref, odd_ref, own_ref, *refs):
    packed_refs = refs[: count - 1]
    taps_out, layers, turned, held = refs[count - 1 :]
    me = group_index()
    column = lax.axis_index("azim")
    lanes = taps_out.shape[2]
    width = taps_out.shape[1]
    per_sweep, rows = own_ref.shape[1], own_ref.shape[0] // 4
    held[0] = own_ref[...]
    for distance in range(1, count):
        held[distance] = packed_refs[distance - 1][: 4 * rows, :]
    for s in range(4):
        for y in range(2):
            slot = slot_of(y * 4 + s, me)
            odd = slot // 4
            block = lax.rem(slot, 4)
            for owner in range(count):
                place = pl.ds(pl.multiple_of((owner ^ column) * rows, rows), rows)
                value = jnp.where(odd == 1, odd_ref[block, place, :], even_ref[block, place, :])
                layers[s, owner * rows : (owner + 1) * rows, y * 2 * lanes : (y + 1) * 2 * lanes] = value[:, : 2 * lanes]
    for s in range(4):
        cots = [held[owner ^ column, s * rows : (s + 1) * rows, :] for owner in range(count)]
        wide = jnp.concatenate(cots, axis=0).astype(F32).T
        for i in (-1, 0, 1):
            moved = wide if i == 0 else pltpu.roll(wide, i % wide.shape[1], 1)
            turned[i + 1, s * per_sweep : (s + 1) * per_sweep, :] = moved.astype(BF)
    for i in (-1, 0, 1):
        for j in (-1, 0, 1):
            found = None
            for s in range(4):
                if 0 <= s - j < 4:
                    part = dot(turned[i + 1, (s - j) * per_sweep : (s - j + 1) * per_sweep, :], layers[s])
                    found = part if found is None else found + part
            for k in (-1, 0, 1):
                tap = None
                for b in range(4):
                    if 0 <= b + k < 4:
                        part = found[b * width : (b + 1) * width, (b + k) * lanes : (b + k + 1) * lanes]
                        tap = part if tap is None else tap + part
                taps_out[9 * (i + 1) + 3 * (j + 1) + (k + 1)] = tap


def last_kernel(count, own_piece, base_ref, taps_ref, *refs):
    come_refs = refs[: count - 1]
    features_out, weights_out = refs[count - 1 :]
    beams, cols, channels = base_ref.shape
    rows = beams * cols
    total = base_ref[...].reshape(rows, channels)
    piece = own_piece[0].astype(F32)
    start = rows * (channels // LANES)
    for ref in come_refs:
        total = total + jnp.concatenate(
            [ref[half * rows : (half + 1) * rows, :].astype(F32) for half in range(channels // LANES)], axis=1
        )
        piece = piece + ref[start:, :].astype(F32)
    features_out[...] = jnp.stack([total[b * cols : (b + 1) * cols] for b in range(beams)], axis=1).astype(BF)
    width, lanes = weights_out.shape[1:]
    for index in range(4):
        weights_out[index] = piece[
            (index % 2) * width : (index % 2 + 1) * width, (index // 2) * lanes : (index // 2 + 1) * lanes
        ]
    weights_out[4:] = taps_ref[...]


def in_hbm(value):
    return pltpu.with_memory_space_constraint(value, pltpu.HBM)


def swap_columns(value, distance):
    count = lax.axis_size("azim")
    return lax.ppermute(value, "azim", [(i, i ^ distance) for i in range(count)])


def exchange(values):
    come = {distance: swap_columns(values[distance], distance) for distance in sorted(values, reverse=True)}
    return [come[distance] for distance in sorted(values)]


def swap(value, bits):
    return lax.ppermute(value, GROUP, [(i, i ^ bits) for i in range(8)])


def add(left, right):
    return (left.astype(F32) + right.astype(F32)).astype(BF)


def per_device(features, cotangent, w_query, w_key, w_value, w_out, w_conv, sector_mask):
    cols, sweeps, beams, channels = features.shape
    count = lax.axis_size("azim")
    assert sweeps == 1 and beams == 2 and cols == SECTOR
    assert lax.axis_size("beam") == 2 and lax.axis_size("sweep") == 4
    width = channels // 8
    lanes = channels // count
    block = (beams, cols, channels)
    whole = (beams, count * cols, channels)

    token = (cols, beams, channels)
    square = (channels, channels)
    own_features, own_cot, allowed, w_query, w_key, w_value, w_out = call(
        functools.partial(prep_kernel, count),
        [(block, BF), (block, BF), ((8, count * cols), F32)] + [(square, BF)] * 4,
        [HBM] * 7,
        scratch=[
            pltpu.VMEM(token, BF),
            pltpu.VMEM(token, BF),
            pltpu.VMEM(sector_mask.shape, jnp.int32),
            pltpu.SemaphoreType.DMA((7,)),
        ],
    )(*map(in_hbm, (features.reshape(token), cotangent.reshape(token), sector_mask, w_query, w_key, w_value, w_out)))
    distances = range(1, count)
    all_features = [own_features] + exchange({distance: own_features for distance in distances})
    even = jnp.stack([own_cot] + [swap(own_cot, bits) for bits in (2, 4, 6)])
    odd = swap(even, 1)

    spread = (4 * cols, 4 * width)
    edge = (8 * beams, channels)
    slices, edges = call(slices_kernel, [(spread, BF), ((2,) + edge, BF)], [VMEM] * 2)(even, odd)
    neighbours = exchange({distance: edges for distance in neighbour_distances(count)})

    pieces_shape = (count, cols, max(LANES, beams * lanes))
    every, queries, keys, values, attended, pieces, w_conv = call(
        functools.partial(forward_kernel, count),
        [(whole, BF), (block, BF), (whole, BF), (whole, BF), (block, BF), (pieces_shape, BF),
         ((TAPS,) + square, BF)],
        [VMEM] * (count + 5) + [HBM],
        scratch=[pltpu.SemaphoreType.DMA],
    )(allowed, *all_features, w_query, w_key, w_value, w_out, in_hbm(w_conv.transpose(1, 0, 2)))

    packed = exchange({distance: jnp.concatenate([slices, pieces[distance]]) for distance in distances})
    layer_block = jnp.concatenate([pieces[0]] + [part[4 * cols :] for part in packed])

    grad_layer, grad_layer_bf, grad_attended = call(
        functools.partial(conv_kernel, count),
        [(block, F32), (block, BF), (block, BF)],
        [VMEM] * (4 + len(neighbours)),
        scratch=[
            pltpu.VMEM((3, beams + 2, cols + 16, channels), F32),
            pltpu.VMEM((2,) + edge, F32),
            pltpu.VMEM((3, 3, (beams + 2) * cols, channels), BF),
        ],
    )(even, odd, *neighbours, w_conv, w_out)

    quarter = (4, 4 * width * channels // LANES, LANES)
    base, send, keep, give = call(
        functools.partial(backward_kernel, count),
        [(block, F32), ((count - 1, beams * cols * channels // LANES, LANES), BF), (quarter, BF), (quarter, BF)],
        [VMEM] * 12,
        scratch=[
            pltpu.VMEM(block, BF),
            pltpu.VMEM(whole, BF),
            pltpu.VMEM(whole, BF),
            pltpu.VMEM((4, 8, width, channels), BF),
        ],
    )(
        allowed, every, queries, keys, values, attended, grad_attended, grad_layer_bf, grad_layer,
        w_query, w_key, w_value,
    )

    sums = add(keep, swap(give, 1))
    both = [swap(jnp.concatenate([layer_block, sums[bits // 2]]), bits) for bits in (2, 4, 6)]
    even_layers = jnp.stack([layer_block] + [part[: layer_block.shape[0]] for part in both])
    odd_layers = swap(even_layers, 1)
    sum_pieces = call(
        functools.partial(pieces_kernel, count),
        [((count, 2 * width, max(LANES, 2 * lanes)), BF)],
        [VMEM] * 4,
    )(sums[0], *both)[0]
    come = exchange({distance: jnp.concatenate([send[distance - 1], sum_pieces[distance]]) for distance in distances})

    taps = call(
        functools.partial(taps_kernel, count),
        [((TAPS, width, lanes), F32)],
        [VMEM] * (2 + count),
        scratch=[
            pltpu.VMEM((4, count * cols, 4 * lanes), BF),
            pltpu.VMEM((3, 16 * width, count * cols), BF),
            pltpu.VMEM((count,) + spread, BF),
        ],
    )(even_layers, odd_layers, slices, *packed)[0]
    features_grad, weight_grads = call(
        functools.partial(last_kernel, count),
        [((cols, beams, channels), BF), ((4 + TAPS, width, lanes), F32)],
        [VMEM] * (2 + count),
    )(sum_pieces, base, taps, *come)
    return features_grad.reshape(features.shape), weight_grads.transpose(2, 0, 1)


def solution(mesh):
    token = P("azim", "sweep", "beam", None)
    in_specs = (token, token, P(), P(), P(), P(), P(), P())
    out_specs = (token, P("azim", None, ("beam", "sweep")))
    return jax.shard_map(per_device, mesh=mesh, in_specs=in_specs, out_specs=out_specs, check_vma=False)
```

```python
import functools

import jax
import jax.numpy as jnp
from jax import lax
from jax.experimental import pallas as pl
from jax.experimental.pallas import tpu as pltpu
from jax.sharding import PartitionSpec as P

HEADS = 8
SECTOR = 64
LANES = 128
TAPS = 27
MASKED = -1e30
GROUP = ("beam", "sweep")

NN = ((1,), (0,))
NT = ((1,), (1,))
TN = ((0,), (0,))

VMEM = pl.BlockSpec(memory_space=pltpu.VMEM)
HBM = pl.BlockSpec(memory_space=pltpu.HBM)
BF = jnp.bfloat16
F32 = jnp.float32


def dot(left, right, dims=NN):
    return lax.dot_general(left, right, (dims, ((), ())), preferred_element_type=F32)


def call(kernel, outs, in_specs, scratch=(), limit=40, micros=2):
    return pl.pallas_call(
        kernel,
        cost_estimate=pl.CostEstimate(flops=int(micros * 1e9), bytes_accessed=0, transcendentals=0),
        out_shape=[jax.ShapeDtypeStruct(shape, dtype) for shape, dtype in outs],
        in_specs=in_specs,
        out_specs=[VMEM] * len(outs),
        scratch_shapes=list(scratch),
        compiler_params=pltpu.CompilerParams(vmem_limit_bytes=limit << 20),
    )


def slot_of(other, own):
    differ = other ^ own
    return (differ & 1) * 4 + (differ >> 1)


def group_index():
    return lax.axis_index("beam") * lax.axis_size("sweep") + lax.axis_index("sweep")


def prep_kernel(count, features_hbm, cot_hbm, mask_hbm, *refs):
    weights_hbm = refs[:4]
    features_out, cot_out, allowed_out = refs[4:7]
    weights_out = refs[7:11]
    features, cot, mask, sems = refs[11:]
    copies = [
        pltpu.make_async_copy(source, target, sems.at[index])
        for index, (source, target) in enumerate(
            zip((features_hbm, cot_hbm, mask_hbm) + weights_hbm, (features, cot, mask) + weights_out)
        )
    ]
    for copy in copies:
        copy.start()
    for copy, source, target in ((copies[0], features, features_out), (copies[1], cot, cot_out)):
        copy.wait()
        wide = source[...].astype(F32)
        for b in range(wide.shape[1]):
            target[b] = wide[:, b, :].astype(BF)
    copies[2].wait()
    me = lax.axis_index("azim")
    square = mask[...].astype(F32)
    row = lax.broadcasted_iota(jnp.int32, square.shape, 0)
    own = jnp.sum(jnp.where(row == me, square, 0.0), axis=0, keepdims=True)
    keys = allowed_out.shape[1]
    sector = lax.broadcasted_iota(jnp.int32, (count, keys), 0)
    block = lax.broadcasted_iota(jnp.int32, (count, keys), 1) // SECTOR
    spread = jnp.where(sector == block ^ me, 1.0, 0.0).astype(BF)
    allowed_out[...] = dot(jnp.broadcast_to(own, (8, count)).astype(BF), spread)
    for copy in copies[3:]:
        copy.wait()


def slices_kernel(even_ref, odd_ref, slices_out, edges_out):
    me = group_index()
    _, beams, cols, channels = even_ref.shape
    width = channels // 8
    for side, col in enumerate((0, cols - 1)):
        base = col // 16 * 16
        rows = []
        for ref in (even_ref, odd_ref):
            for block in range(4):
                for b in range(beams):
                    part = ref[block, b, base : base + 16, :].astype(F32)
                    rows.append(part[col - base : col - base + 1])
        edges_out[side] = jnp.concatenate(rows, axis=0).astype(BF)
    channel = lax.broadcasted_iota(jnp.int32, (channels, 4 * width), 0) - width * me
    lane = lax.broadcasted_iota(jnp.int32, (channels, 4 * width), 1)
    total = [None] * 4
    for b in range(4):
        pick = jnp.where(channel + width * b == lane, 1.0, 0.0)
        pick = jnp.where((channel >= 0) & (channel < width), pick, 0.0).astype(BF)
        for s in range(4):
            slot = slot_of((b // beams) * 4 + s, me)
            odd = slot // 4
            block = lax.rem(slot, 4)
            value = jnp.where(odd == 1, odd_ref[block, b % beams], even_ref[block, b % beams])
            part = dot(value, pick)
            total[s] = part if total[s] is None else total[s] + part
    for s in range(4):
        slices_out[cols * s : cols * (s + 1), :] = total[s].astype(BF)


def neighbour_distances(count):
    return [distance for distance in range(1, count) if distance & (distance + 1) == 0]


def conv_kernel(count, even_ref, odd_ref, *refs):
    distances = neighbour_distances(count)
    edge_refs = refs[: len(distances)]
    w_low_ref, w_high_ref, w_out_ref, layer_out, layer_bf_out, attended_out, padded, edges, shifted = refs[len(distances) :]
    me = group_index()
    column = lax.axis_index("azim")
    sweep = lax.axis_index("sweep")
    beam = lax.axis_index("beam")
    _, beams, cols, channels = even_ref.shape
    for index, step in enumerate((count - 1, 1)):
        partner = lax.rem(column + step, count) ^ column
        total = None
        for distance, ref in zip(distances, edge_refs):
            part = ref[1 - index].astype(F32) * jnp.where(partner == distance, 1.0, 0.0)
            total = part if total is None else total + part
        edges[index] = total
    for j in range(3):
        other_sweep = sweep + (j - 1)
        sweep_ok = (other_sweep >= 0) & (other_sweep < 4)
        for m in range(beams + 2):
            other_beam = beam + (-1 if m == 0 else (1 if m == beams + 1 else 0))
            within = (m - 1) % beams
            ok = sweep_ok & (other_beam >= 0) & (other_beam < 2)
            keep = jnp.where(ok, 1.0, 0.0)
            other = jnp.where(ok, other_beam * 4 + other_sweep, me)
            slot = slot_of(other, me)
            odd = slot // 4
            block = lax.rem(slot, 4)
            value = jnp.where(odd == 1, odd_ref[block, within], even_ref[block, within])
            padded[j, m, 8 : 8 + cols, :] = value.astype(F32) * keep
            row = slot * beams + within
            padded[j, m, 7:8, :] = edges[0, pl.ds(row, 1), :] * keep
            padded[j, m, 8 + cols : 9 + cols, :] = edges[1, pl.ds(row, 1), :] * keep
    for i in (-1, 0, 1):
        for j in range(3):
            for m in range(beams + 2):
                shifted[i + 1, j, m * cols : (m + 1) * cols, :] = padded[j, m, 8 - i : 8 - i + cols, :].astype(BF)
    total = even_ref[0].reshape(beams * cols, channels).astype(F32)
    for i in (-1, 0, 1):
        for j in (-1, 0, 1):
            for k in (-1, 0, 1):
                rows = shifted[i + 1, 1 - j, (1 - k) * cols : (1 - k + beams) * cols, :]
                tap = 9 * (i + 1) + 3 * (j + 1) + (k + 1)
                low = w_low_ref.shape[0]
                w_tap = w_low_ref[tap] if tap < low else w_high_ref[tap - low]
                total = total + dot(rows, w_tap, NT)
    rounded = total.astype(BF)
    layer_out[...] = total.reshape(beams, cols, channels)
    layer_bf_out[...] = rounded.reshape(beams, cols, channels)
    attended_out[...] = dot(rounded, w_out_ref[...], NT).astype(BF).reshape(beams, cols, channels)


def by_head(rows):
    cols, channels = rows.shape
    head = lax.broadcasted_iota(jnp.int32, rows.shape, 1) // (channels // HEADS)
    wide = rows.astype(F32)
    return jnp.concatenate([jnp.where(head == h, wide, 0.0).astype(BF) for h in range(HEADS)], axis=0)


def own_head(stacked):
    cols = stacked.shape[0] // HEADS
    channels = stacked.shape[1]
    head = lax.broadcasted_iota(jnp.int32, (cols, channels), 1) // (channels // HEADS)
    total = jnp.zeros((cols, channels), F32)
    for h in range(HEADS):
        total = jnp.where(head == h, stacked[h * cols : (h + 1) * cols], total)
    return total


def weights_of(queries_by_head, keys, allowed):
    scale = (queries_by_head.shape[1] // HEADS) ** (-0.5)
    scores = jnp.where(allowed, dot(queries_by_head, keys, NT) * scale, MASKED)
    peak = jnp.max(scores, axis=-1, keepdims=True)
    logsum = peak + jnp.log(jnp.sum(jnp.exp(scores - peak), axis=-1, keepdims=True))
    return jnp.where(allowed, jnp.exp(scores - logsum), 0.0)


def project_kernel(count, *refs):
    feature_refs = refs[:count]
    w_query, w_key, w_value, w_conv_hbm, all_out, query_out, key_out, value_out, w_conv_out, sem = refs[count:]
    copy = pltpu.make_async_copy(w_conv_hbm.at[: w_conv_out.shape[0]], w_conv_out, sem)
    copy.start()
    beams, cols, channels = feature_refs[0].shape
    for ahead in range(count):
        all_out[:, ahead * cols : (ahead + 1) * cols, :] = feature_refs[ahead][...]
    own = feature_refs[0][...].reshape(beams * cols, channels)
    every = all_out[...].reshape(beams * count * cols, channels)
    query_out[...] = dot(own, w_query[...]).astype(BF).reshape(beams, cols, channels)
    key_out[...] = dot(every, w_key[...]).astype(BF).reshape(beams, count * cols, channels)
    value_out[...] = dot(every, w_value[...]).astype(BF).reshape(beams, count * cols, channels)
    copy.wait()


def stack_kernel(after_ref, *refs):
    out = refs[-1]
    for index, ref in enumerate(refs[:-1]):
        out[index] = ref[...]


def attention_kernel(count, allowed_ref, own_ref, query_ref, key_ref, value_ref, w_out, w_conv_hbm,
                     attended_out, pieces_out, w_conv_out, sem):
    copy = pltpu.make_async_copy(w_conv_hbm.at[TAPS - w_conv_out.shape[0] :], w_conv_out, sem)
    copy.start()
    beams, cols, channels = query_ref.shape
    allowed = allowed_ref[0:1, :] > 0.5
    for b in range(beams):
        weights = weights_of(by_head(query_ref[b]), key_ref[b], allowed)
        attended_out[b] = own_head(dot(weights.astype(BF), value_ref[b])).astype(BF)
    own = own_ref[...].reshape(beams * cols, channels)
    mixed = own.astype(F32) + dot(attended_out[...].reshape(beams * cols, channels), w_out[...])
    me = lax.axis_index("azim")
    width = channels // count
    for owner in range(count):
        part = [mixed[b * cols : (b + 1) * cols, owner * width : (owner + 1) * width] for b in range(beams)]
        spare = pieces_out.shape[2] - beams * width
        if spare:
            part.append(jnp.zeros((cols, spare), F32))
        pieces_out[owner ^ me] = jnp.concatenate(part, axis=1).astype(BF)
    copy.wait()


def backward_kernel(count, allowed_ref, all_ref, query_ref, key_ref, value_ref, attended_ref, grad_ref, layer_bf_ref,
                    layer_ref, w_query, w_key, w_value, base_out, send_out, keep_out, *refs):
    *pass_outs, grad_query, grad_key, grad_value, sums = refs
    beams, cols, channels = query_ref.shape
    scale = (channels // HEADS) ** (-0.5)
    allowed = allowed_ref[0:1, :] > 0.5
    for b in range(beams):
        queries = by_head(query_ref[b])
        keys = key_ref[b]
        weights = weights_of(queries, keys, allowed)
        grads = by_head(grad_ref[b])
        attended = jnp.concatenate([attended_ref[b].astype(F32)] * HEADS, axis=0)
        delta = jnp.sum(grads.astype(F32) * attended, axis=-1, keepdims=True)
        grad_score = (weights * (dot(grads, value_ref[b], NT) - delta)).astype(BF)
        grad_query[b] = (own_head(dot(grad_score, keys)) * scale).astype(BF)
        grad_key[b] = (dot(grad_score, queries, TN) * scale).astype(BF)
        grad_value[b] = dot(weights.astype(BF), grads, TN).astype(BF)
    own_rows = beams * cols
    all_rows = beams * count * cols
    query_flat = grad_query[...].reshape(own_rows, channels)
    key_flat = grad_key[...].reshape(all_rows, channels)
    value_flat = grad_value[...].reshape(all_rows, channels)
    own = dot(query_flat, w_query[...], NT).reshape(beams, cols, channels) + layer_ref[...]
    spread = dot(key_flat, w_key[...], NT) + dot(value_flat, w_value[...], NT)
    spread = spread.reshape(beams, count, cols, channels)
    base_out[...] = own + spread[:, 0]
    for ahead in range(1, count):
        part = spread[:, ahead].astype(BF).reshape(beams * cols, channels)
        for half in range(channels // LANES):
            send_out[ahead - 1, half * beams * cols : (half + 1) * beams * cols, :] = part[
                :, half * LANES : (half + 1) * LANES
            ]
    every = all_ref[...].reshape(all_rows, channels)
    mine = all_ref[:, :cols, :].reshape(own_rows, channels)
    width = channels // 8
    for index, (left, right) in enumerate(
        (
            (query_flat, mine),
            (key_flat, every),
            (value_flat, every),
            (layer_bf_ref[...].reshape(own_rows, channels), attended_ref[...].reshape(own_rows, channels)),
        )
    ):
        sums[index] = dot(left, right, TN).astype(BF).reshape(8, width, channels)
    me = group_index()
    for differ in range(8):
        target = pass_outs[differ >> 1] if differ & 1 else keep_out.at[differ >> 1]
        for index in range(4):
            part = sums[index, me ^ differ]
            for half in range(channels // LANES):
                row = (half * 4 + index) * width
                target[row : row + width, :] = part[:, half * LANES : (half + 1) * LANES]


def pack_kernel(keep_ref, layer_ref, send_ref, *refs):
    come_refs = refs[:4]
    mine_out, *give_outs, send_out = refs[4:]
    rows = layer_ref.shape[0]
    for block, ref in enumerate(come_refs):
        total = (keep_ref[block].astype(F32) + ref[...].astype(F32)).astype(BF)
        if block == 0:
            mine_out[...] = total
        else:
            give_outs[block - 1][:rows, :] = layer_ref[...]
            give_outs[block - 1][rows:, :] = total
    send_out[...] = send_ref[...]


def pieces_kernel(count, keep_ref, *refs):
    pieces_out = refs[-1]
    me = lax.axis_index("azim")
    rows = keep_ref.shape[0]
    total = keep_ref[...].astype(F32)
    for ref in refs[:-1]:
        total = total + ref[ref.shape[0] - rows :, :].astype(F32)
    halves = 2
    rows = rows // halves
    total = jnp.concatenate([total[half * rows : (half + 1) * rows] for half in range(halves)], axis=1)
    width = total.shape[1] // count
    half = rows // 2
    for owner in range(count):
        part = total[:, owner * width : (owner + 1) * width]
        part = [part[:half], part[half:]]
        spare = pieces_out.shape[2] - 2 * width
        if spare:
            part.append(jnp.zeros((half, spare), F32))
        pieces_out[owner ^ me] = jnp.concatenate(part, axis=1).astype(BF)


def taps_kernel(count, even_ref, odd_ref, own_ref, *refs):
    packed_refs = refs[: count - 1]
    taps_out, layers, turned, held = refs[count - 1 :]
    me = group_index()
    column = lax.axis_index("azim")
    lanes = taps_out.shape[2]
    width = taps_out.shape[1]
    per_sweep, rows = own_ref.shape[1], own_ref.shape[0] // 4
    held[0] = own_ref[...]
    for distance in range(1, count):
        held[distance] = packed_refs[distance - 1][: 4 * rows, :]
    for s in range(4):
        for y in range(2):
            slot = slot_of(y * 4 + s, me)
            odd = slot // 4
            block = lax.rem(slot, 4)
            for owner in range(count):
                place = pl.ds(pl.multiple_of((owner ^ column) * rows, rows), rows)
                value = jnp.where(odd == 1, odd_ref[block, place, :], even_ref[block, place, :])
                layers[s, owner * rows : (owner + 1) * rows, y * 2 * lanes : (y + 1) * 2 * lanes] = value[:, : 2 * lanes]
    for s in range(4):
        cots = [held[owner ^ column, s * rows : (s + 1) * rows, :] for owner in range(count)]
        wide = jnp.concatenate(cots, axis=0).astype(F32).T
        for i in (-1, 0, 1):
            moved = wide if i == 0 else pltpu.roll(wide, i % wide.shape[1], 1)
            turned[i + 1, s * per_sweep : (s + 1) * per_sweep, :] = moved.astype(BF)
    for i in (-1, 0, 1):
        for j in (-1, 0, 1):
            found = None
            for s in range(4):
                if 0 <= s - j < 4:
                    part = dot(turned[i + 1, (s - j) * per_sweep : (s - j + 1) * per_sweep, :], layers[s])
                    found = part if found is None else found + part
            for k in (-1, 0, 1):
                tap = None
                for b in range(4):
                    if 0 <= b + k < 4:
                        part = found[b * width : (b + 1) * width, (b + k) * lanes : (b + k + 1) * lanes]
                        tap = part if tap is None else tap + part
                taps_out[9 * (i + 1) + 3 * (j + 1) + (k + 1)] = tap


def last_kernel(count, own_piece, base_ref, taps_ref, *refs):
    grad_refs, piece_refs = refs[: count - 1], refs[count - 1 : 2 * count - 2]
    features_out, weights_out = refs[2 * count - 2 :]
    beams, cols, channels = base_ref.shape
    rows = beams * cols
    total = base_ref[...].reshape(rows, channels)
    piece = own_piece[0].astype(F32)
    for ref in grad_refs:
        total = total + jnp.concatenate(
            [ref[half * rows : (half + 1) * rows, :].astype(F32) for half in range(channels // LANES)], axis=1
        )
    for ref in piece_refs:
        piece = piece + ref[...].astype(F32)
    features_out[...] = jnp.stack([total[b * cols : (b + 1) * cols] for b in range(beams)], axis=1).astype(BF)
    width, lanes = weights_out.shape[1:]
    for index in range(4):
        weights_out[index] = piece[
            (index % 2) * width : (index % 2 + 1) * width, (index // 2) * lanes : (index // 2 + 1) * lanes
        ]
    weights_out[4:] = taps_ref[...]


def in_hbm(value):
    return pltpu.with_memory_space_constraint(value, pltpu.HBM)


def swap_columns(value, distance):
    count = lax.axis_size("azim")
    return lax.ppermute(value, "azim", [(i, i ^ distance) for i in range(count)])


def exchange(values):
    come = {distance: swap_columns(values[distance], distance) for distance in sorted(values, reverse=True)}
    return [come[distance] for distance in sorted(values)]


def swap(value, bits):
    return lax.ppermute(value, GROUP, [(i, i ^ bits) for i in range(8)])


def per_device(features, cotangent, w_query, w_key, w_value, w_out, w_conv, sector_mask):
    cols, sweeps, beams, channels = features.shape
    count = lax.axis_size("azim")
    assert sweeps == 1 and beams == 2 and cols == SECTOR
    assert lax.axis_size("beam") == 2 and lax.axis_size("sweep") == 4
    width = channels // 8
    lanes = channels // count
    block = (beams, cols, channels)
    whole = (beams, count * cols, channels)

    token = (cols, beams, channels)
    square = (channels, channels)
    own_features, own_cot, allowed, w_query, w_key, w_value, w_out = call(
        functools.partial(prep_kernel, count),
        [(block, BF), (block, BF), ((8, count * cols), F32)] + [(square, BF)] * 4,
        [HBM] * 7,
        scratch=[
            pltpu.VMEM(token, BF),
            pltpu.VMEM(token, BF),
            pltpu.VMEM(sector_mask.shape, jnp.int32),
            pltpu.SemaphoreType.DMA((7,)),
        ],
    )(*map(in_hbm, (features.reshape(token), cotangent.reshape(token), sector_mask, w_query, w_key, w_value, w_out)))
    distances = range(1, count)
    all_features = [own_features] + exchange({distance: own_features for distance in distances})
    low = TAPS // 2
    taps_hbm = in_hbm(w_conv.transpose(1, 0, 2))
    every, queries, keys, values, w_low = call(
        functools.partial(project_kernel, count),
        [(whole, BF), (block, BF), (whole, BF), (whole, BF), ((low,) + square, BF)],
        [VMEM] * (count + 3) + [HBM],
        scratch=[pltpu.SemaphoreType.DMA],
    )(*all_features, w_query, w_key, w_value, taps_hbm)

    even = call(stack_kernel, [((4,) + block, BF)], [VMEM] * 5)(
        queries, own_cot, *[swap(own_cot, bits) for bits in (2, 4, 6)]
    )[0]
    odd = swap(even, 1)

    pieces_shape = (count, cols, max(LANES, beams * lanes))
    attended, pieces, w_high = call(
        functools.partial(attention_kernel, count),
        [(block, BF), (pieces_shape, BF), ((TAPS - low,) + square, BF)],
        [VMEM] * 6 + [HBM],
        scratch=[pltpu.SemaphoreType.DMA],
    )(allowed, own_features, queries, keys, values, w_out, taps_hbm)

    spread = (4 * cols, 4 * width)
    edge = (8 * beams, channels)
    slices, edges = call(slices_kernel, [(spread, BF), ((2,) + edge, BF)], [VMEM] * 2)(even, odd)
    neighbours = exchange({distance: edges for distance in neighbour_distances(count)})

    packed = exchange({distance: jnp.concatenate([slices, pieces[distance]]) for distance in distances})
    layer_block = jnp.concatenate([pieces[0]] + [part[4 * cols :] for part in packed])

    grad_layer, grad_layer_bf, grad_attended = call(
        functools.partial(conv_kernel, count),
        [(block, F32), (block, BF), (block, BF)],
        [VMEM] * (5 + len(neighbours)),
        scratch=[
            pltpu.VMEM((3, beams + 2, cols + 16, channels), F32),
            pltpu.VMEM((2,) + edge, F32),
            pltpu.VMEM((3, 3, (beams + 2) * cols, channels), BF),
        ],
    )(even, odd, *neighbours, w_low, w_high, w_out)

    quarter = (4, 4 * width * channels // LANES, LANES)
    base, send, keep, *gives = call(
        functools.partial(backward_kernel, count),
        [(block, F32), ((count - 1, beams * cols * channels // LANES, LANES), BF), (quarter, BF)] + [(quarter[1:], BF)] * 4,
        [VMEM] * 12,
        scratch=[
            pltpu.VMEM(block, BF),
            pltpu.VMEM(whole, BF),
            pltpu.VMEM(whole, BF),
            pltpu.VMEM((4, 8, width, channels), BF),
        ],
    )(
        allowed, every, queries, keys, values, attended, grad_attended, grad_layer_bf, grad_layer,
        w_query, w_key, w_value,
    )

    rows = quarter[1] + layer_block.shape[0]
    mine, *gives, send = call(
        pack_kernel, [(quarter[1:], BF)] + [((rows, LANES), BF)] * 3 + [(send.shape, BF)], [VMEM] * 7
    )(keep, layer_block, send, *[swap(give, 1) for give in gives])
    both = [swap(give, bits) for give, bits in zip(gives, (2, 4, 6))]
    come_grads = exchange({distance: send[distance - 1] for distance in distances})
    even_layers = jnp.stack([layer_block] + [part[: layer_block.shape[0]] for part in both])
    odd_layers = swap(even_layers, 1)
    sum_pieces = call(
        functools.partial(pieces_kernel, count),
        [((count, 2 * width, max(LANES, 2 * lanes)), BF)],
        [VMEM] * 4,
    )(mine, *both)[0]
    come_pieces = exchange({distance: sum_pieces[distance] for distance in distances})

    taps = call(
        functools.partial(taps_kernel, count),
        [((TAPS, width, lanes), F32)],
        [VMEM] * (2 + count),
        scratch=[
            pltpu.VMEM((4, count * cols, 4 * lanes), BF),
            pltpu.VMEM((3, 16 * width, count * cols), BF),
            pltpu.VMEM((count,) + spread, BF),
        ],
    )(even_layers, odd_layers, slices, *packed)[0]
    features_grad, weight_grads = call(
        functools.partial(last_kernel, count),
        [((cols, beams, channels), BF), ((4 + TAPS, width, lanes), F32)],
        [VMEM] * (1 + 2 * count),
    )(sum_pieces, base, taps, *come_grads, *come_pieces)
    return features_grad.reshape(features.shape), weight_grads.transpose(2, 0, 1)


def solution(mesh):
    token = P("azim", "sweep", "beam", None)
    in_specs = (token, token, P(), P(), P(), P(), P(), P())
    out_specs = (token, P("azim", None, ("beam", "sweep")))
    return jax.shard_map(per_device, mesh=mesh, in_specs=in_specs, out_specs=out_specs, check_vma=False)
```

```python
import functools

import jax
import jax.numpy as jnp
from jax import lax
from jax.experimental import pallas as pl
from jax.experimental.pallas import tpu as pltpu
from jax.sharding import PartitionSpec as P

HEADS = 8
SECTOR = 64
LANES = 128
TAPS = 27
MASKED = -1e30
GROUP = ("beam", "sweep")

NN = ((1,), (0,))
NT = ((1,), (1,))
TN = ((0,), (0,))

VMEM = pl.BlockSpec(memory_space=pltpu.VMEM)
HBM = pl.BlockSpec(memory_space=pltpu.HBM)
BF = jnp.bfloat16
F32 = jnp.float32


def dot(left, right, dims=NN):
    return lax.dot_general(left, right, (dims, ((), ())), preferred_element_type=F32)


def call(kernel, outs, in_specs, out_specs=None, scratch=(), aliases=None, limit=40, micros=2):
    return pl.pallas_call(
        kernel,
        cost_estimate=pl.CostEstimate(flops=int(micros * 1e9), bytes_accessed=0, transcendentals=0),
        out_shape=[jax.ShapeDtypeStruct(shape, dtype) for shape, dtype in outs],
        in_specs=in_specs,
        out_specs=out_specs or [VMEM] * len(outs),
        input_output_aliases=aliases or {},
        scratch_shapes=list(scratch),
        compiler_params=pltpu.CompilerParams(vmem_limit_bytes=limit << 20),
    )


def slot_of(other, own):
    differ = other ^ own
    return (differ & 1) * 4 + (differ >> 1)


def group_index():
    return lax.axis_index("beam") * lax.axis_size("sweep") + lax.axis_index("sweep")


def allowed_row(mask, count, keys):
    me = lax.axis_index("azim")
    square = mask.astype(F32)
    row = lax.broadcasted_iota(jnp.int32, square.shape, 0)
    own = jnp.sum(jnp.where(row == me, square, 0.0), axis=0, keepdims=True)
    sector = lax.broadcasted_iota(jnp.int32, (count, keys), 0)
    block = lax.broadcasted_iota(jnp.int32, (count, keys), 1) // SECTOR
    spread = jnp.where(sector == block ^ me, 1.0, 0.0).astype(BF)
    return dot(jnp.broadcast_to(own, (8, count)).astype(BF), spread)


def slices_kernel(even_ref, odd_ref, slices_out, edges_out):
    me = group_index()
    _, beams, cols, channels = even_ref.shape
    width = channels // 8
    for side, col in enumerate((0, cols - 1)):
        base = col // 16 * 16
        rows = []
        for ref in (even_ref, odd_ref):
            for block in range(4):
                for b in range(beams):
                    part = ref[block, b, base : base + 16, :].astype(F32)
                    rows.append(part[col - base : col - base + 1])
        edges_out[side] = jnp.concatenate(rows, axis=0).astype(BF)
    channel = lax.broadcasted_iota(jnp.int32, (channels, 4 * width), 0) - width * me
    lane = lax.broadcasted_iota(jnp.int32, (channels, 4 * width), 1)
    total = [None] * 4
    for b in range(4):
        pick = jnp.where(channel + width * b == lane, 1.0, 0.0)
        pick = jnp.where((channel >= 0) & (channel < width), pick, 0.0).astype(BF)
        for s in range(4):
            slot = slot_of((b // beams) * 4 + s, me)
            odd = slot // 4
            block = lax.rem(slot, 4)
            value = jnp.where(odd == 1, odd_ref[block, b % beams], even_ref[block, b % beams])
            part = dot(value, pick)
            total[s] = part if total[s] is None else total[s] + part
    for s in range(4):
        slices_out[cols * s : cols * (s + 1), :] = total[s].astype(BF)


def neighbour_distances(count):
    return [distance for distance in range(1, count) if distance & (distance + 1) == 0]


def conv_kernel(count, even_ref, odd_ref, *refs):
    distances = neighbour_distances(count)
    edge_refs = refs[: len(distances)]
    w_ref, w_out_ref, layer_out, layer_bf_out, attended_out, padded, edges, shifted = refs[len(distances) :]
    me = group_index()
    column = lax.axis_index("azim")
    sweep = lax.axis_index("sweep")
    beam = lax.axis_index("beam")
    _, beams, cols, channels = even_ref.shape
    for index, step in enumerate((count - 1, 1)):
        partner = lax.rem(column + step, count) ^ column
        total = None
        for distance, ref in zip(distances, edge_refs):
            part = ref[1 - index].astype(F32) * jnp.where(partner == distance, 1.0, 0.0)
            total = part if total is None else total + part
        edges[index] = total
    for j in range(3):
        other_sweep = sweep + (j - 1)
        sweep_ok = (other_sweep >= 0) & (other_sweep < 4)
        for m in range(beams + 2):
            other_beam = beam + (-1 if m == 0 else (1 if m == beams + 1 else 0))
            within = (m - 1) % beams
            ok = sweep_ok & (other_beam >= 0) & (other_beam < 2)
            keep = jnp.where(ok, 1.0, 0.0)
            other = jnp.where(ok, other_beam * 4 + other_sweep, me)
            slot = slot_of(other, me)
            odd = slot // 4
            block = lax.rem(slot, 4)
            value = jnp.where(odd == 1, odd_ref[block, within], even_ref[block, within])
            padded[j, m, 8 : 8 + cols, :] = value.astype(F32) * keep
            row = slot * beams + within
            padded[j, m, 7:8, :] = edges[0, pl.ds(row, 1), :] * keep
            padded[j, m, 8 + cols : 9 + cols, :] = edges[1, pl.ds(row, 1), :] * keep
    for i in (-1, 0, 1):
        for j in range(3):
            for m in range(beams + 2):
                shifted[i + 1, j, m * cols : (m + 1) * cols, :] = padded[j, m, 8 - i : 8 - i + cols, :].astype(BF)
    total = even_ref[0].reshape(beams * cols, channels).astype(F32)
    for i in (-1, 0, 1):
        for j in (-1, 0, 1):
            for k in (-1, 0, 1):
                rows = shifted[i + 1, 1 - j, (1 - k) * cols : (1 - k + beams) * cols, :]
                tap = 9 * (i + 1) + 3 * (j + 1) + (k + 1)
                total = total + dot(rows, w_ref[tap], NT)
    rounded = total.astype(BF)
    layer_out[...] = total.reshape(beams, cols, channels)
    layer_bf_out[...] = rounded.reshape(beams, cols, channels)
    attended_out[...] = dot(rounded, w_out_ref[...], NT).astype(BF).reshape(beams, cols, channels)


def by_head(rows):
    cols, channels = rows.shape
    head = lax.broadcasted_iota(jnp.int32, rows.shape, 1) // (channels // HEADS)
    wide = rows.astype(F32)
    return jnp.concatenate([jnp.where(head == h, wide, 0.0).astype(BF) for h in range(HEADS)], axis=0)


def own_head(stacked):
    cols = stacked.shape[0] // HEADS
    channels = stacked.shape[1]
    head = lax.broadcasted_iota(jnp.int32, (cols, channels), 1) // (channels // HEADS)
    total = jnp.zeros((cols, channels), F32)
    for h in range(HEADS):
        total = jnp.where(head == h, stacked[h * cols : (h + 1) * cols], total)
    return total


def weights_of(queries_by_head, keys, allowed):
    scale = (queries_by_head.shape[1] // HEADS) ** (-0.5)
    scores = jnp.where(allowed, dot(queries_by_head, keys, NT) * scale, MASKED)
    peak = jnp.max(scores, axis=-1, keepdims=True)
    logsum = peak + jnp.log(jnp.sum(jnp.exp(scores - peak), axis=-1, keepdims=True))
    return jnp.where(allowed, jnp.exp(scores - logsum), 0.0)


def project_kernel(count, *refs):
    come_refs = refs[: count - 1]
    own_hbm, cot_hbm, *weights_hbm, mask_hbm = refs[count - 1 : count + 6]
    all_out, query_out, key_out, value_out, allowed_out, w_out_out, cot_out = refs[count + 6 : count + 13]
    own, cot, w_query, w_key, w_value, mask, sems = refs[count + 13 :]
    targets = (own, w_key, w_value, w_query, mask, w_out_out, cot)
    sources = (own_hbm, weights_hbm[1], weights_hbm[2], weights_hbm[0], mask_hbm, weights_hbm[3], cot_hbm)
    copies = [
        pltpu.make_async_copy(source, target, sems.at[index])
        for index, (source, target) in enumerate(zip(sources, targets))
    ]
    for copy in copies:
        copy.start()
    cols, beams, channels = own.shape
    for distance in range(1, count):
        all_out[:, distance * cols : (distance + 1) * cols, :] = jnp.swapaxes(come_refs[distance - 1][...], 0, 1)
    copies[0].wait()
    all_out[:, :cols, :] = jnp.swapaxes(own[...], 0, 1)
    every = all_out[...].reshape(beams * count * cols, channels)
    copies[1].wait()
    key_out[...] = dot(every, w_key[...]).astype(BF).reshape(beams, count * cols, channels)
    copies[2].wait()
    value_out[...] = dot(every, w_value[...]).astype(BF).reshape(beams, count * cols, channels)
    copies[3].wait()
    mine = all_out[:, :cols, :].reshape(beams * cols, channels)
    query_out[...] = dot(mine, w_query[...]).astype(BF).reshape(beams, cols, channels)
    copies[4].wait()
    allowed_out[...] = allowed_row(mask[...], count, count * cols)
    copies[5].wait()
    copies[6].wait()
    cot_out[...] = jnp.swapaxes(cot[...], 0, 1)


def stack_kernel(own_ref, *refs):
    *come_refs, out = refs
    out[0] = own_ref[...]
    for index, ref in enumerate(come_refs, 1):
        out[index] = jnp.swapaxes(ref[...], 0, 1)


def attention_kernel(count, allowed_ref, all_ref, query_ref, key_ref, value_ref, w_out,
                     attended_out, pieces_out, weights_out):
    beams, cols, channels = query_ref.shape
    allowed = allowed_ref[0:1, :] > 0.5
    for b in range(beams):
        weights = weights_of(by_head(query_ref[b]), key_ref[b], allowed)
        weights_out[b] = weights
        attended_out[b] = own_head(dot(weights.astype(BF), value_ref[b])).astype(BF)
    own = all_ref[:, :cols, :].reshape(beams * cols, channels)
    mixed = own.astype(F32) + dot(attended_out[...].reshape(beams * cols, channels), w_out[...])
    me = lax.axis_index("azim")
    width = channels // count
    for owner in range(count):
        part = [mixed[b * cols : (b + 1) * cols, owner * width : (owner + 1) * width] for b in range(beams)]
        spare = pieces_out.shape[2] - beams * width
        if spare:
            part.append(jnp.zeros((cols, spare), F32))
        pieces_out[owner ^ me] = jnp.concatenate(part, axis=1).astype(BF)


def backward_kernel(count, weights_ref, all_ref, query_ref, key_ref, value_ref, attended_ref, grad_ref, layer_bf_ref,
                    layer_ref, w_query, w_key, w_value, base_out, send_out, keep_out, *refs):
    *pass_outs, grad_query, grad_key, grad_value, sums = refs
    beams, cols, channels = query_ref.shape
    scale = (channels // HEADS) ** (-0.5)
    for b in range(beams):
        queries = by_head(query_ref[b])
        keys = key_ref[b]
        weights = weights_ref[b]
        grads = by_head(grad_ref[b])
        attended = jnp.concatenate([attended_ref[b].astype(F32)] * HEADS, axis=0)
        delta = jnp.sum(grads.astype(F32) * attended, axis=-1, keepdims=True)
        grad_score = (weights * (dot(grads, value_ref[b], NT) - delta)).astype(BF)
        grad_query[b] = (own_head(dot(grad_score, keys)) * scale).astype(BF)
        grad_key[b] = (dot(grad_score, queries, TN) * scale).astype(BF)
        grad_value[b] = dot(weights.astype(BF), grads, TN).astype(BF)
    own_rows = beams * cols
    all_rows = beams * count * cols
    query_flat = grad_query[...].reshape(own_rows, channels)
    key_flat = grad_key[...].reshape(all_rows, channels)
    value_flat = grad_value[...].reshape(all_rows, channels)
    own = dot(query_flat, w_query[...], NT).reshape(beams, cols, channels) + layer_ref[...]
    spread = dot(key_flat, w_key[...], NT) + dot(value_flat, w_value[...], NT)
    spread = spread.reshape(beams, count, cols, channels)
    base_out[...] = own + spread[:, 0]
    for ahead in range(1, count):
        part = spread[:, ahead].astype(BF).reshape(beams * cols, channels)
        for half in range(channels // LANES):
            send_out[ahead - 1, half * beams * cols : (half + 1) * beams * cols, :] = part[
                :, half * LANES : (half + 1) * LANES
            ]
    every = all_ref[...].reshape(all_rows, channels)
    mine = all_ref[:, :cols, :].reshape(own_rows, channels)
    width = channels // 8
    for index, (left, right) in enumerate(
        (
            (query_flat, mine),
            (key_flat, every),
            (value_flat, every),
            (layer_bf_ref[...].reshape(own_rows, channels), attended_ref[...].reshape(own_rows, channels)),
        )
    ):
        sums[index] = dot(left, right, TN).astype(BF).reshape(8, width, channels)
    me = group_index()
    for differ in range(8):
        target = pass_outs[differ >> 1] if differ & 1 else keep_out.at[differ >> 1]
        for index in range(4):
            part = sums[index, me ^ differ]
            for half in range(channels // LANES):
                row = (half * 4 + index) * width
                target[row : row + width, :] = part[:, half * LANES : (half + 1) * LANES]


def pack_kernel(keep_ref, layer_ref, send_ref, *refs):
    come_refs = refs[:4]
    mine_out, *give_outs, send_out = refs[4:]
    rows = layer_ref.shape[0]
    for block, ref in enumerate(come_refs):
        total = (keep_ref[block].astype(F32) + ref[...].astype(F32)).astype(BF)
        if block == 0:
            mine_out[...] = total
        else:
            give_outs[block - 1][:rows, :] = layer_ref[...]
            give_outs[block - 1][rows:, :] = total
    send_out[...] = send_ref[...]


def pieces_kernel(count, keep_ref, *refs):
    pieces_out = refs[-1]
    me = lax.axis_index("azim")
    rows = keep_ref.shape[0]
    total = keep_ref[...].astype(F32)
    for ref in refs[:-1]:
        total = total + ref[ref.shape[0] - rows :, :].astype(F32)
    halves = 2
    rows = rows // halves
    total = jnp.concatenate([total[half * rows : (half + 1) * rows] for half in range(halves)], axis=1)
    width = total.shape[1] // count
    half = rows // 2
    for owner in range(count):
        part = total[:, owner * width : (owner + 1) * width]
        part = [part[:half], part[half:]]
        spare = pieces_out.shape[2] - 2 * width
        if spare:
            part.append(jnp.zeros((half, spare), F32))
        pieces_out[owner ^ me] = jnp.concatenate(part, axis=1).astype(BF)


def taps_kernel(count, even_ref, odd_ref, own_ref, *refs):
    packed_refs = refs[: count - 1]
    taps_out, layers, turned, held = refs[count - 1 :]
    me = group_index()
    column = lax.axis_index("azim")
    lanes = taps_out.shape[2]
    width = taps_out.shape[1]
    per_sweep, rows = own_ref.shape[1], own_ref.shape[0] // 4
    held[0] = own_ref[...]
    for distance in range(1, count):
        held[distance] = packed_refs[distance - 1][: 4 * rows, :]
    for s in range(4):
        for y in range(2):
            slot = slot_of(y * 4 + s, me)
            odd = slot // 4
            block = lax.rem(slot, 4)
            for owner in range(count):
                place = pl.ds(pl.multiple_of((owner ^ column) * rows, rows), rows)
                value = jnp.where(odd == 1, odd_ref[block, place, :], even_ref[block, place, :])
                layers[s, owner * rows : (owner + 1) * rows, y * 2 * lanes : (y + 1) * 2 * lanes] = value[:, : 2 * lanes]
    for s in range(4):
        cots = [held[owner ^ column, s * rows : (s + 1) * rows, :] for owner in range(count)]
        wide = jnp.concatenate(cots, axis=0).astype(F32).T
        for i in (-1, 0, 1):
            moved = wide if i == 0 else pltpu.roll(wide, i % wide.shape[1], 1)
            turned[i + 1, s * per_sweep : (s + 1) * per_sweep, :] = moved.astype(BF)
    for i in (-1, 0, 1):
        for j in (-1, 0, 1):
            found = None
            for s in range(4):
                if 0 <= s - j < 4:
                    part = dot(turned[i + 1, (s - j) * per_sweep : (s - j + 1) * per_sweep, :], layers[s])
                    found = part if found is None else found + part
            for k in (-1, 0, 1):
                tap = None
                for b in range(4):
                    if 0 <= b + k < 4:
                        part = found[b * width : (b + 1) * width, (b + k) * lanes : (b + k + 1) * lanes]
                        tap = part if tap is None else tap + part
                taps_out[9 * (i + 1) + 3 * (j + 1) + (k + 1)] = tap


def last_kernel(count, own_piece, base_ref, taps_ref, *refs):
    grad_refs, piece_refs = refs[: count - 1], refs[count - 1 : 2 * count - 2]
    features_out, weights_out = refs[2 * count - 2 :]
    beams, cols, channels = base_ref.shape
    rows = beams * cols
    total = base_ref[...].reshape(rows, channels)
    piece = own_piece[0].astype(F32)
    for ref in grad_refs:
        total = total + jnp.concatenate(
            [ref[half * rows : (half + 1) * rows, :].astype(F32) for half in range(channels // LANES)], axis=1
        )
    for ref in piece_refs:
        piece = piece + ref[...].astype(F32)
    features_out[...] = jnp.swapaxes(total.reshape(beams, cols, channels).astype(BF), 0, 1)
    width, lanes = weights_out.shape[1:]
    for index in range(4):
        weights_out[index] = piece[
            (index % 2) * width : (index % 2 + 1) * width, (index // 2) * lanes : (index // 2 + 1) * lanes
        ]
    weights_out[4:] = taps_ref[...]


def in_hbm(value):
    return pltpu.with_memory_space_constraint(value, pltpu.HBM)


def swap_columns(value, distance):
    count = lax.axis_size("azim")
    return lax.ppermute(value, "azim", [(i, i ^ distance) for i in range(count)])


def exchange(values):
    come = {distance: swap_columns(values[distance], distance) for distance in sorted(values, reverse=True)}
    return [come[distance] for distance in sorted(values)]


def swap(value, bits):
    return lax.ppermute(value, GROUP, [(i, i ^ bits) for i in range(8)])


def per_device(features, cotangent, w_query, w_key, w_value, w_out, w_conv, sector_mask):
    cols, sweeps, beams, channels = features.shape
    count = lax.axis_size("azim")
    assert sweeps == 1 and beams == 2 and cols == SECTOR
    assert lax.axis_size("beam") == 2 and lax.axis_size("sweep") == 4
    width = channels // 8
    lanes = channels // count
    block = (beams, cols, channels)
    whole = (beams, count * cols, channels)

    token = (cols, beams, channels)
    square = (channels, channels)
    distances = range(1, count)
    raw_features, raw_cot = features.reshape(token), cotangent.reshape(token)
    come_features = exchange({distance: raw_features for distance in distances})
    come_cot = [swap(raw_cot, bits) for bits in (2, 4, 6)]

    every, queries, keys, values, allowed, w_out, own_cot = call(
        functools.partial(project_kernel, count),
        [(whole, BF), (block, BF), (whole, BF), (whole, BF), ((8, count * cols), F32), (square, BF), (block, BF)],
        [VMEM] * (count - 1) + [HBM] * 7,
        scratch=[pltpu.VMEM(token, BF)] * 2 + [pltpu.VMEM(square, BF)] * 3
        + [pltpu.VMEM(sector_mask.shape, jnp.int32), pltpu.SemaphoreType.DMA((7,))],
    )(*come_features, *map(in_hbm, (raw_features, raw_cot, w_query, w_key, w_value, w_out, sector_mask)))

    even = call(stack_kernel, [((4,) + block, BF)], [VMEM] * 4)(own_cot, *come_cot)[0]
    odd = swap(even, 1)

    pieces_shape = (count, cols, max(LANES, beams * lanes))
    attended, pieces, weights = call(
        functools.partial(attention_kernel, count),
        [(block, BF), (pieces_shape, BF), ((beams, HEADS * cols, count * cols), F32)],
        [VMEM] * 6,
    )(allowed, every, queries, keys, values, w_out)

    spread = (4 * cols, 4 * width)
    edge = (8 * beams, channels)
    slices, edges = call(slices_kernel, [(spread, BF), ((2,) + edge, BF)], [VMEM] * 2)(even, odd)
    neighbours = exchange({distance: edges for distance in neighbour_distances(count)})

    packed = exchange({distance: jnp.concatenate([slices, pieces[distance]]) for distance in distances})
    layer_block = jnp.concatenate([pieces[0]] + [part[4 * cols :] for part in packed])

    grad_layer, grad_layer_bf, grad_attended = call(
        functools.partial(conv_kernel, count),
        [(block, F32), (block, BF), (block, BF)],
        [VMEM] * (4 + len(neighbours)),
        scratch=[
            pltpu.VMEM((3, beams + 2, cols + 16, channels), F32),
            pltpu.VMEM((2,) + edge, F32),
            pltpu.VMEM((3, 3, (beams + 2) * cols, channels), BF),
        ],
    )(even, odd, *neighbours, w_conv.transpose(1, 0, 2), w_out)

    quarter = (4, 4 * width * channels // LANES, LANES)
    base, send, keep, *gives = call(
        functools.partial(backward_kernel, count),
        [(block, F32), ((count - 1, beams * cols * channels // LANES, LANES), BF), (quarter, BF)] + [(quarter[1:], BF)] * 4,
        [VMEM] * 12,
        scratch=[
            pltpu.VMEM(block, BF),
            pltpu.VMEM(whole, BF),
            pltpu.VMEM(whole, BF),
            pltpu.VMEM((4, 8, width, channels), BF),
        ],
    )(
        weights, every, queries, keys, values, attended, grad_attended, grad_layer_bf, grad_layer,
        w_query, w_key, w_value,
    )

    rows = quarter[1] + layer_block.shape[0]
    mine, *gives, send = call(
        pack_kernel, [(quarter[1:], BF)] + [((rows, LANES), BF)] * 3 + [(send.shape, BF)], [VMEM] * 7
    )(keep, layer_block, send, *[swap(give, 1) for give in gives])
    both = [swap(give, bits) for give, bits in zip(gives, (2, 4, 6))]
    come_grads = exchange({distance: send[distance - 1] for distance in distances})
    even_layers = jnp.stack([layer_block] + [part[: layer_block.shape[0]] for part in both])
    odd_layers = swap(even_layers, 1)
    sum_pieces = call(
        functools.partial(pieces_kernel, count),
        [((count, 2 * width, max(LANES, 2 * lanes)), BF)],
        [VMEM] * 4,
    )(mine, *both)[0]
    come_pieces = exchange({distance: sum_pieces[distance] for distance in distances})

    taps = call(
        functools.partial(taps_kernel, count),
        [((TAPS, width, lanes), F32)],
        [VMEM] * (2 + count),
        scratch=[
            pltpu.VMEM((4, count * cols, 4 * lanes), BF),
            pltpu.VMEM((3, 16 * width, count * cols), BF),
            pltpu.VMEM((count,) + spread, BF),
        ],
    )(even_layers, odd_layers, slices, *packed)[0]
    features_grad, weight_grads = call(
        functools.partial(last_kernel, count),
        [((cols, beams, channels), BF), ((4 + TAPS, width, lanes), F32)],
        [VMEM] * (1 + 2 * count),
    )(sum_pieces, base, taps, *come_grads, *come_pieces)
    return features_grad.reshape(features.shape), weight_grads.transpose(2, 0, 1)


def solution(mesh):
    token = P("azim", "sweep", "beam", None)
    in_specs = (token, token, P(), P(), P(), P(), P(), P())
    out_specs = (token, P("azim", None, ("beam", "sweep")))
    return jax.shard_map(per_device, mesh=mesh, in_specs=in_specs, out_specs=out_specs, check_vma=False)
```

```python
import functools

import jax
import jax.numpy as jnp
from jax import lax
from jax.experimental import pallas as pl
from jax.experimental.pallas import tpu as pltpu
from jax.sharding import PartitionSpec as P

HEADS = 8
SECTOR = 64
LANES = 128
TAPS = 27
MASKED = -1e30
GROUP = ("beam", "sweep")

NN = ((1,), (0,))
NT = ((1,), (1,))
TN = ((0,), (0,))

VMEM = pl.BlockSpec(memory_space=pltpu.VMEM)
HBM = pl.BlockSpec(memory_space=pltpu.HBM)
BF = jnp.bfloat16
F32 = jnp.float32


def dot(left, right, dims=NN):
    return lax.dot_general(left, right, (dims, ((), ())), preferred_element_type=F32)


def call(kernel, outs, in_specs, out_specs=None, scratch=(), aliases=None, limit=40, micros=2):
    return pl.pallas_call(
        kernel,
        cost_estimate=pl.CostEstimate(flops=int(micros * 1e9), bytes_accessed=0, transcendentals=0),
        out_shape=[jax.ShapeDtypeStruct(shape, dtype) for shape, dtype in outs],
        in_specs=in_specs,
        out_specs=out_specs or [VMEM] * len(outs),
        input_output_aliases=aliases or {},
        scratch_shapes=list(scratch),
        compiler_params=pltpu.CompilerParams(vmem_limit_bytes=limit << 20),
    )


def slot_of(other, own):
    differ = other ^ own
    return (differ & 1) * 4 + (differ >> 1)


def group_index():
    return lax.axis_index("beam") * lax.axis_size("sweep") + lax.axis_index("sweep")


def allowed_row(mask, count, keys):
    me = lax.axis_index("azim")
    square = mask.astype(F32)
    row = lax.broadcasted_iota(jnp.int32, square.shape, 0)
    own = jnp.sum(jnp.where(row == me, square, 0.0), axis=0, keepdims=True)
    sector = lax.broadcasted_iota(jnp.int32, (count, keys), 0)
    block = lax.broadcasted_iota(jnp.int32, (count, keys), 1) // SECTOR
    spread = jnp.where(sector == block ^ me, 1.0, 0.0).astype(BF)
    return dot(jnp.broadcast_to(own, (8, count)).astype(BF), spread)


def slices_kernel(even_ref, odd_ref, pieces_ref, slices_out, edges_out, pieces_out):
    pieces_out[...] = pieces_ref[...]
    me = group_index()
    _, beams, cols, channels = even_ref.shape
    width = channels // 8
    for side, col in enumerate((0, cols - 1)):
        base = col // 16 * 16
        rows = []
        for ref in (even_ref, odd_ref):
            for block in range(4):
                for b in range(beams):
                    part = ref[block, b, base : base + 16, :].astype(F32)
                    rows.append(part[col - base : col - base + 1])
        edges_out[side] = jnp.concatenate(rows, axis=0).astype(BF)
    channel = lax.broadcasted_iota(jnp.int32, (channels, 4 * width), 0) - width * me
    lane = lax.broadcasted_iota(jnp.int32, (channels, 4 * width), 1)
    total = [None] * 4
    for b in range(4):
        pick = jnp.where(channel + width * b == lane, 1.0, 0.0)
        pick = jnp.where((channel >= 0) & (channel < width), pick, 0.0).astype(BF)
        for s in range(4):
            slot = slot_of((b // beams) * 4 + s, me)
            odd = slot // 4
            block = lax.rem(slot, 4)
            value = jnp.where(odd == 1, odd_ref[block, b % beams], even_ref[block, b % beams])
            part = dot(value, pick)
            total[s] = part if total[s] is None else total[s] + part
    for s in range(4):
        slices_out[cols * s : cols * (s + 1), :] = total[s].astype(BF)


def neighbour_distances(count):
    return [distance for distance in range(1, count) if distance & (distance + 1) == 0]


def conv_kernel(count, even_ref, odd_ref, *refs):
    distances = neighbour_distances(count)
    edge_refs = refs[: len(distances)]
    w_ref, w_out_ref, layer_out, layer_bf_out, attended_out, main, edges, halo = refs[len(distances) :]
    me = group_index()
    column = lax.axis_index("azim")
    sweep = lax.axis_index("sweep")
    beam = lax.axis_index("beam")
    _, beams, cols, channels = even_ref.shape
    for index, step in enumerate((count - 1, 1)):
        partner = lax.rem(column + step, count) ^ column
        total = None
        for distance, ref in zip(distances, edge_refs):
            part = ref[1 - index].astype(F32) * jnp.where(partner == distance, 1.0, 0.0)
            total = part if total is None else total + part
        edges[index] = total
    for j in range(3):
        other_sweep = sweep + (j - 1)
        sweep_ok = (other_sweep >= 0) & (other_sweep < 4)
        for m in range(beams + 2):
            other_beam = beam + (-1 if m == 0 else (1 if m == beams + 1 else 0))
            within = (m - 1) % beams
            ok = sweep_ok & (other_beam >= 0) & (other_beam < 2)
            keep = jnp.where(ok, 1.0, 0.0)
            other = jnp.where(ok, other_beam * 4 + other_sweep, me)
            slot = slot_of(other, me)
            odd = slot // 4
            block = lax.rem(slot, 4)
            value = jnp.where(odd == 1, odd_ref[block, within], even_ref[block, within])
            main[j, m * cols : (m + 1) * cols, :] = (value.astype(F32) * keep).astype(BF)
            row = slot * beams + within
            for side in range(2):
                halo[side, j, m : m + 1, :] = edges[side, pl.ds(row, 1), :] * keep
    rows = beams * cols
    total = even_ref[0].reshape(rows, channels).astype(F32)
    spare = jnp.zeros((16 - beams, channels), F32)
    for i in (0, 1, -1):
        found = None
        for j in (-1, 0, 1):
            for k in (-1, 0, 1):
                left = main[1 - j, (1 - k) * cols : (1 - k + beams) * cols, :]
                if i:
                    edge = halo[0 if i == 1 else 1, 1 - j, 1 - k : 1 - k + beams, :]
                    left = jnp.concatenate([left, jnp.concatenate([edge, spare]).astype(BF)])
                part = dot(w_ref[9 * (i + 1) + 3 * (j + 1) + (k + 1)], left, NT)
                found = part if found is None else found + part
        found = found.T
        if i == 1:
            parts = [[found[rows + b : rows + b + 1], found[b * cols : (b + 1) * cols - 1]] for b in range(beams)]
        elif i == -1:
            parts = [[found[b * cols + 1 : (b + 1) * cols], found[rows + b : rows + b + 1]] for b in range(beams)]
        else:
            parts = [[found]]
        total = total + jnp.concatenate([part for pair in parts for part in pair], axis=0)
    rounded = total.astype(BF)
    layer_out[...] = total.reshape(beams, cols, channels)
    layer_bf_out[...] = rounded.reshape(beams, cols, channels)
    attended_out[...] = dot(rounded, w_out_ref[...], NT).astype(BF).reshape(beams, cols, channels)


def by_head(rows):
    cols, channels = rows.shape
    head = lax.broadcasted_iota(jnp.int32, rows.shape, 1) // (channels // HEADS)
    wide = rows.astype(F32)
    return jnp.concatenate([jnp.where(head == h, wide, 0.0).astype(BF) for h in range(HEADS)], axis=0)


def own_head(stacked):
    cols = stacked.shape[0] // HEADS
    channels = stacked.shape[1]
    head = lax.broadcasted_iota(jnp.int32, (cols, channels), 1) // (channels // HEADS)
    total = jnp.zeros((cols, channels), F32)
    for h in range(HEADS):
        total = jnp.where(head == h, stacked[h * cols : (h + 1) * cols], total)
    return total


def weights_of(queries_by_head, keys, allowed):
    scale = (queries_by_head.shape[1] // HEADS) ** (-0.5)
    scores = jnp.where(allowed, dot(queries_by_head, keys, NT) * scale, MASKED)
    peak = jnp.max(scores, axis=-1, keepdims=True)
    logsum = peak + jnp.log(jnp.sum(jnp.exp(scores - peak), axis=-1, keepdims=True))
    return jnp.where(allowed, jnp.exp(scores - logsum), 0.0)


def load_kernel(count, *refs):
    own_hbm, cot_hbm, mask_hbm, *weights_hbm = refs[:7]
    own_out, cot_out, allowed_out, *weights_out = refs[7:14]
    own, cot, mask, sems = refs[14:]
    copies = [
        pltpu.make_async_copy(source, target, sems.at[index])
        for index, (source, target) in enumerate(
            zip((own_hbm, cot_hbm, mask_hbm, *weights_hbm), (own, cot, mask, *weights_out))
        )
    ]
    for copy in copies:
        copy.start()
    for copy in copies:
        copy.wait()
    own_out[...] = jnp.swapaxes(own[...], 0, 1)
    cot_out[...] = jnp.swapaxes(cot[...], 0, 1)
    allowed_out[...] = allowed_row(mask[...], count, allowed_out.shape[1])


def project_kernel(count, *refs):
    own_ref, *come_refs = refs[:count]
    w_query, w_key, w_value, all_out, query_out, key_out, value_out = refs[count:]
    beams, cols, channels = own_ref.shape
    for distance in range(1, count):
        all_out[:, distance * cols : (distance + 1) * cols, :] = jnp.swapaxes(come_refs[distance - 1][...], 0, 1)
    all_out[:, :cols, :] = own_ref[...]
    every = all_out[...].reshape(beams * count * cols, channels)
    key_out[...] = dot(every, w_key[...]).astype(BF).reshape(beams, count * cols, channels)
    value_out[...] = dot(every, w_value[...]).astype(BF).reshape(beams, count * cols, channels)
    mine = all_out[:, :cols, :].reshape(beams * cols, channels)
    query_out[...] = dot(mine, w_query[...]).astype(BF).reshape(beams, cols, channels)


def stack_kernel(after_ref, own_ref, *refs):
    *come_refs, out = refs
    out[0] = own_ref[...]
    for index, ref in enumerate(come_refs, 1):
        out[index] = jnp.swapaxes(ref[...], 0, 1)


def attention_kernel(count, allowed_ref, all_ref, query_ref, key_ref, value_ref, w_out,
                     attended_out, pieces_out, weights_out):
    beams, cols, channels = query_ref.shape
    allowed = allowed_ref[0:1, :] > 0.5
    for b in range(beams):
        weights = weights_of(by_head(query_ref[b]), key_ref[b], allowed)
        weights_out[b] = weights
        attended_out[b] = own_head(dot(weights.astype(BF), value_ref[b])).astype(BF)
    own = all_ref[:, :cols, :].reshape(beams * cols, channels)
    mixed = own.astype(F32) + dot(attended_out[...].reshape(beams * cols, channels), w_out[...])
    me = lax.axis_index("azim")
    width = channels // count
    for owner in range(count):
        part = [mixed[b * cols : (b + 1) * cols, owner * width : (owner + 1) * width] for b in range(beams)]
        spare = pieces_out.shape[2] - beams * width
        if spare:
            part.append(jnp.zeros((cols, spare), F32))
        pieces_out[owner ^ me] = jnp.concatenate(part, axis=1).astype(BF)


def backward_kernel(count, weights_ref, all_ref, query_ref, key_ref, value_ref, attended_ref, grad_ref, layer_bf_ref,
                    layer_ref, w_query, w_key, w_value, base_out, send_out, keep_out, *refs):
    *pass_outs, grad_query, grad_key, grad_value, sums = refs
    beams, cols, channels = query_ref.shape
    scale = (channels // HEADS) ** (-0.5)
    for b in range(beams):
        queries = by_head(query_ref[b])
        keys = key_ref[b]
        weights = weights_ref[b]
        grads = by_head(grad_ref[b])
        attended = jnp.concatenate([attended_ref[b].astype(F32)] * HEADS, axis=0)
        delta = jnp.sum(grads.astype(F32) * attended, axis=-1, keepdims=True)
        grad_score = (weights * (dot(grads, value_ref[b], NT) - delta)).astype(BF)
        grad_query[b] = (own_head(dot(grad_score, keys)) * scale).astype(BF)
        grad_key[b] = (dot(grad_score, queries, TN) * scale).astype(BF)
        grad_value[b] = dot(weights.astype(BF), grads, TN).astype(BF)
    own_rows = beams * cols
    all_rows = beams * count * cols
    query_flat = grad_query[...].reshape(own_rows, channels)
    key_flat = grad_key[...].reshape(all_rows, channels)
    value_flat = grad_value[...].reshape(all_rows, channels)
    own = dot(query_flat, w_query[...], NT).reshape(beams, cols, channels) + layer_ref[...]
    spread = dot(key_flat, w_key[...], NT) + dot(value_flat, w_value[...], NT)
    spread = spread.reshape(beams, count, cols, channels)
    base_out[...] = own + spread[:, 0]
    for ahead in range(1, count):
        part = spread[:, ahead].astype(BF).reshape(beams * cols, channels)
        for half in range(channels // LANES):
            send_out[ahead - 1, half * beams * cols : (half + 1) * beams * cols, :] = part[
                :, half * LANES : (half + 1) * LANES
            ]
    every = all_ref[...].reshape(all_rows, channels)
    mine = all_ref[:, :cols, :].reshape(own_rows, channels)
    width = channels // 8
    for index, (left, right) in enumerate(
        (
            (query_flat, mine),
            (key_flat, every),
            (value_flat, every),
            (layer_bf_ref[...].reshape(own_rows, channels), attended_ref[...].reshape(own_rows, channels)),
        )
    ):
        sums[index] = dot(left, right, TN).astype(BF).reshape(8, width, channels)
    me = group_index()
    for differ in range(8):
        target = pass_outs[differ >> 1] if differ & 1 else keep_out.at[differ >> 1]
        for index in range(4):
            part = sums[index, me ^ differ]
            for half in range(channels // LANES):
                row = (half * 4 + index) * width
                target[row : row + width, :] = part[:, half * LANES : (half + 1) * LANES]


def pack_kernel(keep_ref, layer_ref, send_ref, *refs):
    come_refs = refs[:4]
    mine_out, *give_outs, send_out = refs[4:]
    rows = layer_ref.shape[0]
    for block, ref in enumerate(come_refs):
        total = (keep_ref[block].astype(F32) + ref[...].astype(F32)).astype(BF)
        if block == 0:
            mine_out[...] = total
        else:
            give_outs[block - 1][:rows, :] = layer_ref[...]
            give_outs[block - 1][rows:, :] = total
    send_out[...] = send_ref[...]


def pieces_kernel(count, keep_ref, *refs):
    pieces_out = refs[-1]
    me = lax.axis_index("azim")
    rows = keep_ref.shape[0]
    total = keep_ref[...].astype(F32)
    for ref in refs[:-1]:
        total = total + ref[ref.shape[0] - rows :, :].astype(F32)
    halves = 2
    rows = rows // halves
    total = jnp.concatenate([total[half * rows : (half + 1) * rows] for half in range(halves)], axis=1)
    width = total.shape[1] // count
    half = rows // 2
    for owner in range(count):
        part = total[:, owner * width : (owner + 1) * width]
        part = [part[:half], part[half:]]
        spare = pieces_out.shape[2] - 2 * width
        if spare:
            part.append(jnp.zeros((half, spare), F32))
        pieces_out[owner ^ me] = jnp.concatenate(part, axis=1).astype(BF)


def taps_kernel(count, even_ref, odd_ref, own_ref, *refs):
    packed_refs, base_ref, grad_refs = refs[: count - 1], refs[count - 1], refs[count : 2 * count - 1]
    taps_out, features_out, layers, turned, held = refs[2 * count - 1 :]
    beams, cols, channels = base_ref.shape
    rows = beams * cols
    total = base_ref[...].reshape(rows, channels)
    for ref in grad_refs:
        total = total + jnp.concatenate(
            [ref[half * rows : (half + 1) * rows, :].astype(F32) for half in range(channels // LANES)], axis=1
        )
    features_out[...] = jnp.swapaxes(total.reshape(beams, cols, channels).astype(BF), 0, 1)
    me = group_index()
    column = lax.axis_index("azim")
    lanes = taps_out.shape[2]
    width = taps_out.shape[1]
    per_sweep, rows = own_ref.shape[1], own_ref.shape[0] // 4
    held[0] = own_ref[...]
    for distance in range(1, count):
        ref = packed_refs[distance - 1]
        held[distance] = ref[ref.shape[0] - 4 * rows :, :]
    for s in range(4):
        for y in range(2):
            slot = slot_of(y * 4 + s, me)
            odd = slot // 4
            block = lax.rem(slot, 4)
            for owner in range(count):
                place = pl.ds(pl.multiple_of((owner ^ column) * rows, rows), rows)
                value = jnp.where(odd == 1, odd_ref[block, place, :], even_ref[block, place, :])
                layers[s, owner * rows : (owner + 1) * rows, y * 2 * lanes : (y + 1) * 2 * lanes] = value[:, : 2 * lanes]
    for s in range(4):
        cots = [held[owner ^ column, s * rows : (s + 1) * rows, :] for owner in range(count)]
        wide = jnp.concatenate(cots, axis=0).astype(F32).T
        for i in (-1, 0, 1):
            moved = wide if i == 0 else pltpu.roll(wide, i % wide.shape[1], 1)
            turned[i + 1, s * per_sweep : (s + 1) * per_sweep, :] = moved.astype(BF)
    for i in (-1, 0, 1):
        for j in (-1, 0, 1):
            found = None
            for s in range(4):
                if 0 <= s - j < 4:
                    part = dot(turned[i + 1, (s - j) * per_sweep : (s - j + 1) * per_sweep, :], layers[s])
                    found = part if found is None else found + part
            for k in (-1, 0, 1):
                tap = None
                for b in range(4):
                    if 0 <= b + k < 4:
                        part = found[b * width : (b + 1) * width, (b + k) * lanes : (b + k + 1) * lanes]
                        tap = part if tap is None else tap + part
                taps_out[9 * (i + 1) + 3 * (j + 1) + (k + 1)] = tap


def last_kernel(own_piece, taps_ref, *refs):
    *piece_refs, weights_out = refs
    piece = own_piece[0].astype(F32)
    for ref in piece_refs:
        piece = piece + ref[...].astype(F32)
    width, lanes = weights_out.shape[1:]
    for index in range(4):
        weights_out[index] = piece[
            (index % 2) * width : (index % 2 + 1) * width, (index // 2) * lanes : (index // 2 + 1) * lanes
        ]
    weights_out[4:] = taps_ref[...]


def in_hbm(value):
    return pltpu.with_memory_space_constraint(value, pltpu.HBM)


def swap_columns(value, distance):
    count = lax.axis_size("azim")
    return lax.ppermute(value, "azim", [(i, i ^ distance) for i in range(count)])


def exchange(values):
    come = {distance: swap_columns(values[distance], distance) for distance in sorted(values, reverse=True)}
    return [come[distance] for distance in sorted(values)]


def swap(value, bits):
    return lax.ppermute(value, GROUP, [(i, i ^ bits) for i in range(8)])


def per_device(features, cotangent, w_query, w_key, w_value, w_out, w_conv, sector_mask):
    cols, sweeps, beams, channels = features.shape
    count = lax.axis_size("azim")
    assert sweeps == 1 and beams == 2 and cols == SECTOR
    assert lax.axis_size("beam") == 2 and lax.axis_size("sweep") == 4
    width = channels // 8
    lanes = channels // count
    block = (beams, cols, channels)
    whole = (beams, count * cols, channels)

    token = (cols, beams, channels)
    square = (channels, channels)
    distances = range(1, count)
    raw_features, raw_cot = features.reshape(token), cotangent.reshape(token)
    come_features = exchange({distance: raw_features for distance in distances})
    come_cot = [swap(raw_cot, bits) for bits in (2, 4, 6)]

    own_features, own_cot, allowed, w_query, w_key, w_value, w_out = call(
        functools.partial(load_kernel, count),
        [(block, BF), (block, BF), ((8, count * cols), F32)] + [(square, BF)] * 4,
        [HBM] * 7,
        scratch=[pltpu.VMEM(token, BF)] * 2
        + [pltpu.VMEM(sector_mask.shape, jnp.int32), pltpu.SemaphoreType.DMA((7,))],
        micros=2,
    )(*map(in_hbm, (raw_features, raw_cot, sector_mask, w_query, w_key, w_value, w_out)))
    every, queries, keys, values = call(
        functools.partial(project_kernel, count),
        [(whole, BF), (block, BF), (whole, BF), (whole, BF)],
        [VMEM] * (count + 3),
        micros=0.01,
    )(own_features, *come_features, w_query, w_key, w_value)

    even = call(stack_kernel, [((4,) + block, BF)], [VMEM] * 5)(queries, own_cot, *come_cot)[0]
    odd = swap(even, 1)

    pieces_shape = (count, cols, max(LANES, beams * lanes))
    attended, pieces, weights = call(
        functools.partial(attention_kernel, count),
        [(block, BF), (pieces_shape, BF), ((beams, HEADS * cols, count * cols), F32)],
        [VMEM] * 6,
    )(allowed, every, queries, keys, values, w_out)

    spread = (4 * cols, 4 * width)
    edge = (8 * beams, channels)
    slices, edges, pieces = call(
        slices_kernel, [(spread, BF), ((2,) + edge, BF), (pieces_shape, BF)], [VMEM] * 3
    )(even, odd, pieces)
    neighbours = exchange({distance: edges for distance in neighbour_distances(count)})

    far = count - 1
    packed = exchange(
        {
            distance: pieces[distance] if distance == far else jnp.concatenate([pieces[distance], slices])
            for distance in distances
        }
    )
    layer_block = jnp.concatenate([pieces[0]] + [part[:cols] for part in packed])

    grad_layer, grad_layer_bf, grad_attended = call(
        functools.partial(conv_kernel, count),
        [(block, F32), (block, BF), (block, BF)],
        [VMEM] * (4 + len(neighbours)),
        scratch=[
            pltpu.VMEM((3, (beams + 2) * cols, channels), BF),
            pltpu.VMEM((2,) + edge, F32),
            pltpu.VMEM((2, 3, 8, channels), F32),
        ],
    )(even, odd, *neighbours, w_conv.transpose(1, 0, 2), w_out)

    quarter = (4, 4 * width * channels // LANES, LANES)
    base, send, keep, *gives = call(
        functools.partial(backward_kernel, count),
        [(block, F32), ((count - 1, beams * cols * channels // LANES, LANES), BF), (quarter, BF)] + [(quarter[1:], BF)] * 4,
        [VMEM] * 12,
        scratch=[
            pltpu.VMEM(block, BF),
            pltpu.VMEM(whole, BF),
            pltpu.VMEM(whole, BF),
            pltpu.VMEM((4, 8, width, channels), BF),
        ],
    )(
        weights, every, queries, keys, values, attended, grad_attended, grad_layer_bf, grad_layer,
        w_query, w_key, w_value,
    )

    rows = quarter[1] + layer_block.shape[0]
    mine, *gives, send = call(
        pack_kernel, [(quarter[1:], BF)] + [((rows, LANES), BF)] * 3 + [(send.shape, BF)], [VMEM] * 7
    )(keep, layer_block, send, *[swap(give, 1) for give in gives])
    both = [swap(give, bits) for give, bits in zip(gives, (2, 4, 6))]
    relayed = packed[far - 2][cols:]
    come_grads = exchange(
        {
            distance: jnp.concatenate([send[distance - 1], relayed]) if distance == 1 else send[distance - 1]
            for distance in distances
        }
    )
    held_slices = packed[: far - 1] + [come_grads[0]]
    even_layers = jnp.stack([layer_block] + [part[: layer_block.shape[0]] for part in both])
    odd_layers = swap(even_layers, 1)
    sum_pieces = call(
        functools.partial(pieces_kernel, count),
        [((count, 2 * width, max(LANES, 2 * lanes)), BF)],
        [VMEM] * 4,
    )(mine, *both)[0]
    come_pieces = exchange({distance: sum_pieces[distance] for distance in distances})

    taps, features_grad = call(
        functools.partial(taps_kernel, count),
        [((TAPS, width, lanes), F32), (token, BF)],
        [VMEM] * (2 + 2 * count),
        scratch=[
            pltpu.VMEM((4, count * cols, 4 * lanes), BF),
            pltpu.VMEM((3, 16 * width, count * cols), BF),
            pltpu.VMEM((count,) + spread, BF),
        ],
    )(even_layers, odd_layers, slices, *held_slices, base, *come_grads)
    weight_grads = call(last_kernel, [((4 + TAPS, width, lanes), F32)], [VMEM] * (1 + count))(
        sum_pieces, taps, *come_pieces
    )[0]
    return features_grad.reshape(features.shape), weight_grads.transpose(2, 0, 1)


def solution(mesh):
    token = P("azim", "sweep", "beam", None)
    in_specs = (token, token, P(), P(), P(), P(), P(), P())
    out_specs = (token, P("azim", None, ("beam", "sweep")))
    return jax.shard_map(per_device, mesh=mesh, in_specs=in_specs, out_specs=out_specs, check_vma=False)
```

```python
import functools

import jax
import jax.numpy as jnp
from jax import lax
from jax.experimental import pallas as pl
from jax.experimental.pallas import tpu as pltpu
from jax.sharding import PartitionSpec as P

HEADS = 8
SECTOR = 64
LANES = 128
TAPS = 27
MASKED = -1e30
GROUP = ("beam", "sweep")

NN = ((1,), (0,))
NT = ((1,), (1,))
TN = ((0,), (0,))

VMEM = pl.BlockSpec(memory_space=pltpu.VMEM)
HBM = pl.BlockSpec(memory_space=pltpu.HBM)
BF = jnp.bfloat16
F32 = jnp.float32


def dot(left, right, dims=NN):
    return lax.dot_general(left, right, (dims, ((), ())), preferred_element_type=F32)


def call(kernel, outs, in_specs, out_specs=None, scratch=(), aliases=None, limit=40, micros=2):
    return pl.pallas_call(
        kernel,
        cost_estimate=pl.CostEstimate(flops=int(micros * 1e9), bytes_accessed=0, transcendentals=0),
        out_shape=[jax.ShapeDtypeStruct(shape, dtype) for shape, dtype in outs],
        in_specs=in_specs,
        out_specs=out_specs or [VMEM] * len(outs),
        input_output_aliases=aliases or {},
        scratch_shapes=list(scratch),
        compiler_params=pltpu.CompilerParams(vmem_limit_bytes=limit << 20),
    )


def slot_of(other, own):
    differ = other ^ own
    return (differ & 1) * 4 + (differ >> 1)


def group_index():
    return lax.axis_index("beam") * lax.axis_size("sweep") + lax.axis_index("sweep")


def allowed_row(mask, count, keys):
    me = lax.axis_index("azim")
    square = mask.astype(F32)
    row = lax.broadcasted_iota(jnp.int32, square.shape, 0)
    own = jnp.sum(jnp.where(row == me, square, 0.0), axis=0, keepdims=True)
    sector = lax.broadcasted_iota(jnp.int32, (count, keys), 0)
    block = lax.broadcasted_iota(jnp.int32, (count, keys), 1) // SECTOR
    spread = jnp.where(sector == block ^ me, 1.0, 0.0).astype(BF)
    return dot(jnp.broadcast_to(own, (8, count)).astype(BF), spread)


def slices_kernel(even_ref, odd_ref, pieces_ref, slices_out, edges_out, pieces_out):
    pieces_out[...] = pieces_ref[...]
    me = group_index()
    _, beams, cols, channels = even_ref.shape
    width = channels // 8
    for side, col in enumerate((0, cols - 1)):
        base = col // 16 * 16
        rows = []
        for ref in (even_ref, odd_ref):
            for block in range(4):
                for b in range(beams):
                    part = ref[block, b, base : base + 16, :].astype(F32)
                    rows.append(part[col - base : col - base + 1])
        edges_out[side] = jnp.concatenate(rows, axis=0).astype(BF)
    channel = lax.broadcasted_iota(jnp.int32, (channels, 4 * width), 0) - width * me
    lane = lax.broadcasted_iota(jnp.int32, (channels, 4 * width), 1)
    total = [None] * 4
    for b in range(4):
        pick = jnp.where(channel + width * b == lane, 1.0, 0.0)
        pick = jnp.where((channel >= 0) & (channel < width), pick, 0.0).astype(BF)
        for s in range(4):
            slot = slot_of((b // beams) * 4 + s, me)
            odd = slot // 4
            block = lax.rem(slot, 4)
            value = jnp.where(odd == 1, odd_ref[block, b % beams], even_ref[block, b % beams])
            part = dot(value, pick)
            total[s] = part if total[s] is None else total[s] + part
    for s in range(4):
        slices_out[cols * s : cols * (s + 1), :] = total[s].astype(BF)


def neighbour_distances(count):
    return [distance for distance in range(1, count) if distance & (distance + 1) == 0]


def conv_kernel(count, even_ref, odd_ref, *refs):
    distances = neighbour_distances(count)
    edge_refs = refs[: len(distances)]
    w_ref, w_out_ref, layer_out, layer_bf_out, attended_out, main, edges, halo = refs[len(distances) :]
    me = group_index()
    column = lax.axis_index("azim")
    sweep = lax.axis_index("sweep")
    beam = lax.axis_index("beam")
    _, beams, cols, channels = even_ref.shape
    for index, step in enumerate((count - 1, 1)):
        partner = lax.rem(column + step, count) ^ column
        total = None
        for distance, ref in zip(distances, edge_refs):
            part = ref[1 - index].astype(F32) * jnp.where(partner == distance, 1.0, 0.0)
            total = part if total is None else total + part
        edges[index] = total
    for j in range(3):
        other_sweep = sweep + (j - 1)
        sweep_ok = (other_sweep >= 0) & (other_sweep < 4)
        for m in range(beams + 2):
            other_beam = beam + (-1 if m == 0 else (1 if m == beams + 1 else 0))
            within = (m - 1) % beams
            ok = sweep_ok & (other_beam >= 0) & (other_beam < 2)
            keep = jnp.where(ok, 1.0, 0.0)
            other = jnp.where(ok, other_beam * 4 + other_sweep, me)
            slot = slot_of(other, me)
            odd = slot // 4
            block = lax.rem(slot, 4)
            value = jnp.where(odd == 1, odd_ref[block, within], even_ref[block, within])
            main[j, m * cols : (m + 1) * cols, :] = (value.astype(F32) * keep).astype(BF)
            row = slot * beams + within
            for side in range(2):
                halo[side, j, m : m + 1, :] = edges[side, pl.ds(row, 1), :] * keep
    rows = beams * cols
    total = even_ref[0].reshape(rows, channels).astype(F32)
    spare = jnp.zeros((16 - beams, channels), F32)
    for i in (0, 1, -1):
        found = None
        for j in (-1, 0, 1):
            for k in (-1, 0, 1):
                left = main[1 - j, (1 - k) * cols : (1 - k + beams) * cols, :]
                if i:
                    edge = halo[0 if i == 1 else 1, 1 - j, 1 - k : 1 - k + beams, :]
                    left = jnp.concatenate([left, jnp.concatenate([edge, spare]).astype(BF)])
                part = dot(w_ref[9 * (i + 1) + 3 * (j + 1) + (k + 1)], left, NT)
                found = part if found is None else found + part
        found = found.T
        if i == 1:
            parts = [[found[rows + b : rows + b + 1], found[b * cols : (b + 1) * cols - 1]] for b in range(beams)]
        elif i == -1:
            parts = [[found[b * cols + 1 : (b + 1) * cols], found[rows + b : rows + b + 1]] for b in range(beams)]
        else:
            parts = [[found]]
        total = total + jnp.concatenate([part for pair in parts for part in pair], axis=0)
    rounded = total.astype(BF)
    layer_out[...] = total.reshape(beams, cols, channels)
    layer_bf_out[...] = rounded.reshape(beams, cols, channels)
    attended_out[...] = dot(rounded, w_out_ref[...], NT).astype(BF).reshape(beams, cols, channels)


def by_head(rows):
    cols, channels = rows.shape
    head = lax.broadcasted_iota(jnp.int32, rows.shape, 1) // (channels // HEADS)
    wide = rows.astype(F32)
    return jnp.concatenate([jnp.where(head == h, wide, 0.0).astype(BF) for h in range(HEADS)], axis=0)


def own_head(stacked):
    cols = stacked.shape[0] // HEADS
    channels = stacked.shape[1]
    head = lax.broadcasted_iota(jnp.int32, (cols, channels), 1) // (channels // HEADS)
    total = jnp.zeros((cols, channels), F32)
    for h in range(HEADS):
        total = jnp.where(head == h, stacked[h * cols : (h + 1) * cols], total)
    return total


def weights_of(queries_by_head, keys, allowed):
    scale = (queries_by_head.shape[1] // HEADS) ** (-0.5)
    scores = jnp.where(allowed, dot(queries_by_head, keys, NT) * scale, MASKED)
    peak = jnp.max(scores, axis=-1, keepdims=True)
    logsum = peak + jnp.log(jnp.sum(jnp.exp(scores - peak), axis=-1, keepdims=True))
    return jnp.where(allowed, jnp.exp(scores - logsum), 0.0)


def load_kernel(count, *refs):
    own_hbm, cot_hbm, mask_hbm, *weights_hbm = refs[:7]
    own_out, cot_out, allowed_out, *weights_out = refs[7:14]
    own, cot, mask, sems = refs[14:]
    copies = [
        pltpu.make_async_copy(source, target, sems.at[index])
        for index, (source, target) in enumerate(
            zip((own_hbm, cot_hbm, mask_hbm, *weights_hbm), (own, cot, mask, *weights_out))
        )
    ]
    for copy in copies:
        copy.start()
    for copy in copies:
        copy.wait()
    own_out[...] = jnp.swapaxes(own[...], 0, 1)
    cot_out[...] = jnp.swapaxes(cot[...], 0, 1)
    allowed_out[...] = allowed_row(mask[...], count, allowed_out.shape[1])


def project_kernel(count, *refs):
    own_ref, *come_refs = refs[:count]
    w_query, w_key, w_value, all_out, query_out, key_out, value_out = refs[count:]
    beams, cols, channels = own_ref.shape
    for distance in range(1, count):
        all_out[:, distance * cols : (distance + 1) * cols, :] = jnp.swapaxes(come_refs[distance - 1][...], 0, 1)
    all_out[:, :cols, :] = own_ref[...]
    every = all_out[...].reshape(beams * count * cols, channels)
    key_out[...] = dot(every, w_key[...]).astype(BF).reshape(beams, count * cols, channels)
    value_out[...] = dot(every, w_value[...]).astype(BF).reshape(beams, count * cols, channels)
    mine = all_out[:, :cols, :].reshape(beams * cols, channels)
    query_out[...] = dot(mine, w_query[...]).astype(BF).reshape(beams, cols, channels)


def stack_kernel(after_ref, own_ref, *refs):
    *come_refs, out = refs
    out[0] = own_ref[...]
    for index, ref in enumerate(come_refs, 1):
        out[index] = jnp.swapaxes(ref[...], 0, 1)


def attention_kernel(count, allowed_ref, all_ref, query_ref, key_ref, value_ref, w_out,
                     attended_out, pieces_out, weights_out):
    beams, cols, channels = query_ref.shape
    allowed = allowed_ref[0:1, :] > 0.5
    for b in range(beams):
        weights = weights_of(by_head(query_ref[b]), key_ref[b], allowed)
        weights_out[b] = weights
        attended_out[b] = own_head(dot(weights.astype(BF), value_ref[b])).astype(BF)
    own = all_ref[:, :cols, :].reshape(beams * cols, channels)
    mixed = own.astype(F32) + dot(attended_out[...].reshape(beams * cols, channels), w_out[...])
    me = lax.axis_index("azim")
    width = channels // count
    for owner in range(count):
        part = [mixed[b * cols : (b + 1) * cols, owner * width : (owner + 1) * width] for b in range(beams)]
        spare = pieces_out.shape[2] - beams * width
        if spare:
            part.append(jnp.zeros((cols, spare), F32))
        pieces_out[owner ^ me] = jnp.concatenate(part, axis=1).astype(BF)


def backward_kernel(count, weights_ref, all_ref, query_ref, key_ref, value_ref, attended_ref, grad_ref, layer_bf_ref,
                    layer_ref, w_query, w_key, w_value, base_out, send_out, keep_out, *refs):
    *pass_outs, grad_query, grad_key, grad_value, sums = refs
    beams, cols, channels = query_ref.shape
    scale = (channels // HEADS) ** (-0.5)
    for b in range(beams):
        queries = by_head(query_ref[b])
        keys = key_ref[b]
        weights = weights_ref[b]
        grads = by_head(grad_ref[b])
        attended = jnp.concatenate([attended_ref[b].astype(F32)] * HEADS, axis=0)
        delta = jnp.sum(grads.astype(F32) * attended, axis=-1, keepdims=True)
        grad_score = (weights * (dot(grads, value_ref[b], NT) - delta)).astype(BF)
        grad_query[b] = (own_head(dot(grad_score, keys)) * scale).astype(BF)
        grad_key[b] = (dot(grad_score, queries, TN) * scale).astype(BF)
        grad_value[b] = dot(weights.astype(BF), grads, TN).astype(BF)
    own_rows = beams * cols
    all_rows = beams * count * cols
    query_flat = grad_query[...].reshape(own_rows, channels)
    key_flat = grad_key[...].reshape(all_rows, channels)
    value_flat = grad_value[...].reshape(all_rows, channels)
    own = dot(query_flat, w_query[...], NT).reshape(beams, cols, channels) + layer_ref[...]
    spread = dot(key_flat, w_key[...], NT) + dot(value_flat, w_value[...], NT)
    spread = spread.reshape(beams, count, cols, channels)
    base_out[...] = own + spread[:, 0]
    for ahead in range(1, count):
        part = spread[:, ahead].astype(BF).reshape(beams * cols, channels)
        for half in range(channels // LANES):
            send_out[ahead - 1, half * beams * cols : (half + 1) * beams * cols, :] = part[
                :, half * LANES : (half + 1) * LANES
            ]
    every = all_ref[...].reshape(all_rows, channels)
    mine = all_ref[:, :cols, :].reshape(own_rows, channels)
    width = channels // 8
    for index, (left, right) in enumerate(
        (
            (query_flat, mine),
            (key_flat, every),
            (value_flat, every),
            (layer_bf_ref[...].reshape(own_rows, channels), attended_ref[...].reshape(own_rows, channels)),
        )
    ):
        sums[index] = dot(left, right, TN).astype(BF).reshape(8, width, channels)
    me = group_index()
    for differ in range(8):
        target = pass_outs[differ >> 1] if differ & 1 else keep_out.at[differ >> 1]
        for index in range(4):
            part = sums[index, me ^ differ]
            for half in range(channels // LANES):
                row = (half * 4 + index) * width
                target[row : row + width, :] = part[:, half * LANES : (half + 1) * LANES]


def pack_kernel(keep_ref, layer_ref, send_ref, give_ref, *refs):
    come_refs, give_outs, (send_out, give_out) = refs[:3], refs[3:6], refs[6:]
    rows = layer_ref.shape[0]
    for block, (ref, out) in enumerate(zip(come_refs, give_outs), 1):
        out[:rows, :] = layer_ref[...]
        out[rows:, :] = (keep_ref[block].astype(F32) + ref[...].astype(F32)).astype(BF)
    send_out[...] = send_ref[...]
    give_out[...] = give_ref[...]


def pieces_kernel(count, keep_ref, mine_ref, *refs):
    pieces_out = refs[-1]
    me = lax.axis_index("azim")
    rows = keep_ref.shape[1]
    total = keep_ref[0].astype(F32) + mine_ref[...].astype(F32)
    for ref in refs[:-1]:
        total = total + ref[ref.shape[0] - rows :, :].astype(F32)
    halves = 2
    rows = rows // halves
    total = jnp.concatenate([total[half * rows : (half + 1) * rows] for half in range(halves)], axis=1)
    width = total.shape[1] // count
    half = rows // 2
    for owner in range(count):
        part = total[:, owner * width : (owner + 1) * width]
        part = [part[:half], part[half:]]
        spare = pieces_out.shape[2] - 2 * width
        if spare:
            part.append(jnp.zeros((half, spare), F32))
        pieces_out[owner ^ me] = jnp.concatenate(part, axis=1).astype(BF)


def taps_kernel(count, even_ref, odd_ref, own_ref, *refs):
    packed_refs, base_ref, grad_refs = refs[: count - 1], refs[count - 1], refs[count : 2 * count - 1]
    taps_out, features_out, layers, turned, held = refs[2 * count - 1 :]
    beams, cols, channels = base_ref.shape
    rows = beams * cols
    total = base_ref[...].reshape(rows, channels)
    for ref in grad_refs:
        total = total + jnp.concatenate(
            [ref[half * rows : (half + 1) * rows, :].astype(F32) for half in range(channels // LANES)], axis=1
        )
    features_out[...] = jnp.swapaxes(total.reshape(beams, cols, channels).astype(BF), 0, 1)
    me = group_index()
    column = lax.axis_index("azim")
    lanes = taps_out.shape[2]
    width = taps_out.shape[1]
    per_sweep, rows = own_ref.shape[1], own_ref.shape[0] // 4
    held[0] = own_ref[...]
    for distance in range(1, count):
        ref = packed_refs[distance - 1]
        held[distance] = ref[ref.shape[0] - 4 * rows :, :]
    for s in range(4):
        for y in range(2):
            slot = slot_of(y * 4 + s, me)
            odd = slot // 4
            block = lax.rem(slot, 4)
            for owner in range(count):
                place = pl.ds(pl.multiple_of((owner ^ column) * rows, rows), rows)
                value = jnp.where(odd == 1, odd_ref[block, place, :], even_ref[block, place, :])
                layers[s, owner * rows : (owner + 1) * rows, y * 2 * lanes : (y + 1) * 2 * lanes] = value[:, : 2 * lanes]
    for s in range(4):
        cots = [held[owner ^ column, s * rows : (s + 1) * rows, :] for owner in range(count)]
        wide = jnp.concatenate(cots, axis=0).astype(F32).T
        for i in (-1, 0, 1):
            moved = wide if i == 0 else pltpu.roll(wide, i % wide.shape[1], 1)
            turned[i + 1, s * per_sweep : (s + 1) * per_sweep, :] = moved.astype(BF)
    for i in (-1, 0, 1):
        for j in (-1, 0, 1):
            found = None
            for s in range(4):
                if 0 <= s - j < 4:
                    part = dot(turned[i + 1, (s - j) * per_sweep : (s - j + 1) * per_sweep, :], layers[s])
                    found = part if found is None else found + part
            for k in (-1, 0, 1):
                tap = None
                for b in range(4):
                    if 0 <= b + k < 4:
                        part = found[b * width : (b + 1) * width, (b + k) * lanes : (b + k + 1) * lanes]
                        tap = part if tap is None else tap + part
                taps_out[9 * (i + 1) + 3 * (j + 1) + (k + 1)] = tap


def last_kernel(own_piece, taps_ref, *refs):
    *piece_refs, weights_out = refs
    piece = own_piece[0].astype(F32)
    for ref in piece_refs:
        piece = piece + ref[...].astype(F32)
    width, lanes = weights_out.shape[1:]
    for index in range(4):
        weights_out[index] = piece[
            (index % 2) * width : (index % 2 + 1) * width, (index // 2) * lanes : (index // 2 + 1) * lanes
        ]
    weights_out[4:] = taps_ref[...]


def in_hbm(value):
    return pltpu.with_memory_space_constraint(value, pltpu.HBM)


def swap_columns(value, distance):
    count = lax.axis_size("azim")
    return lax.ppermute(value, "azim", [(i, i ^ distance) for i in range(count)])


def exchange(values):
    come = {distance: swap_columns(values[distance], distance) for distance in sorted(values, reverse=True)}
    return [come[distance] for distance in sorted(values)]


def swap(value, bits):
    return lax.ppermute(value, GROUP, [(i, i ^ bits) for i in range(8)])


def per_device(features, cotangent, w_query, w_key, w_value, w_out, w_conv, sector_mask):
    cols, sweeps, beams, channels = features.shape
    count = lax.axis_size("azim")
    assert sweeps == 1 and beams == 2 and cols == SECTOR
    assert lax.axis_size("beam") == 2 and lax.axis_size("sweep") == 4
    width = channels // 8
    lanes = channels // count
    block = (beams, cols, channels)
    whole = (beams, count * cols, channels)

    token = (cols, beams, channels)
    square = (channels, channels)
    distances = range(1, count)
    raw_features, raw_cot = features.reshape(token), cotangent.reshape(token)
    come_features = exchange({distance: raw_features for distance in distances})
    come_cot = [swap(raw_cot, bits) for bits in (2, 4, 6)]

    own_features, own_cot, allowed, w_query, w_key, w_value, w_out = call(
        functools.partial(load_kernel, count),
        [(block, BF), (block, BF), ((8, count * cols), F32)] + [(square, BF)] * 4,
        [HBM] * 7,
        scratch=[pltpu.VMEM(token, BF)] * 2
        + [pltpu.VMEM(sector_mask.shape, jnp.int32), pltpu.SemaphoreType.DMA((7,))],
        micros=2,
    )(*map(in_hbm, (raw_features, raw_cot, sector_mask, w_query, w_key, w_value, w_out)))
    every, queries, keys, values = call(
        functools.partial(project_kernel, count),
        [(whole, BF), (block, BF), (whole, BF), (whole, BF)],
        [VMEM] * (count + 3),
        micros=0.01,
    )(own_features, *come_features, w_query, w_key, w_value)

    even = call(stack_kernel, [((4,) + block, BF)], [VMEM] * 5)(queries, own_cot, *come_cot)[0]
    odd = swap(even, 1)

    pieces_shape = (count, cols, max(LANES, beams * lanes))
    attended, pieces, weights = call(
        functools.partial(attention_kernel, count),
        [(block, BF), (pieces_shape, BF), ((beams, HEADS * cols, count * cols), F32)],
        [VMEM] * 6,
    )(allowed, every, queries, keys, values, w_out)

    spread = (4 * cols, 4 * width)
    edge = (8 * beams, channels)
    slices, edges, pieces = call(
        slices_kernel, [(spread, BF), ((2,) + edge, BF), (pieces_shape, BF)], [VMEM] * 3
    )(even, odd, pieces)
    neighbours = exchange({distance: edges for distance in neighbour_distances(count)})

    far = count - 1
    packed = exchange(
        {
            distance: pieces[distance] if distance == far else jnp.concatenate([pieces[distance], slices])
            for distance in distances
        }
    )
    layer_block = jnp.concatenate([pieces[0]] + [part[:cols] for part in packed])

    grad_layer, grad_layer_bf, grad_attended = call(
        functools.partial(conv_kernel, count),
        [(block, F32), (block, BF), (block, BF)],
        [VMEM] * (4 + len(neighbours)),
        scratch=[
            pltpu.VMEM((3, (beams + 2) * cols, channels), BF),
            pltpu.VMEM((2,) + edge, F32),
            pltpu.VMEM((2, 3, 8, channels), F32),
        ],
    )(even, odd, *neighbours, w_conv.transpose(1, 0, 2), w_out)

    quarter = (4, 4 * width * channels // LANES, LANES)
    base, send, keep, *gives = call(
        functools.partial(backward_kernel, count),
        [(block, F32), ((count - 1, beams * cols * channels // LANES, LANES), BF), (quarter, BF)] + [(quarter[1:], BF)] * 4,
        [VMEM] * 12,
        scratch=[
            pltpu.VMEM(block, BF),
            pltpu.VMEM(whole, BF),
            pltpu.VMEM(whole, BF),
            pltpu.VMEM((4, 8, width, channels), BF),
        ],
    )(
        weights, every, queries, keys, values, attended, grad_attended, grad_layer_bf, grad_layer,
        w_query, w_key, w_value,
    )

    rows = quarter[1] + layer_block.shape[0]
    *packs, send, give = call(
        pack_kernel, [((rows, LANES), BF)] * 3 + [(send.shape, BF), (quarter[1:], BF)], [VMEM] * 7
    )(keep, layer_block, send, gives[0], *[swap(part, 1) for part in gives[1:]])
    mine = swap(give, 1)
    both = [swap(give, bits) for give, bits in zip(packs, (2, 4, 6))]
    relayed = packed[far - 2][cols:]
    come_grads = exchange(
        {
            distance: jnp.concatenate([send[distance - 1], relayed]) if distance == 1 else send[distance - 1]
            for distance in distances
        }
    )
    held_slices = packed[: far - 1] + [come_grads[0]]
    even_layers = jnp.stack([layer_block] + [part[: layer_block.shape[0]] for part in both])
    odd_layers = swap(even_layers, 1)
    sum_pieces = call(
        functools.partial(pieces_kernel, count),
        [((count, 2 * width, max(LANES, 2 * lanes)), BF)],
        [VMEM] * 5,
    )(keep, mine, *both)[0]
    come_pieces = exchange({distance: sum_pieces[distance] for distance in distances})

    taps, features_grad = call(
        functools.partial(taps_kernel, count),
        [((TAPS, width, lanes), F32), (token, BF)],
        [VMEM] * (2 + 2 * count),
        scratch=[
            pltpu.VMEM((4, count * cols, 4 * lanes), BF),
            pltpu.VMEM((3, 16 * width, count * cols), BF),
            pltpu.VMEM((count,) + spread, BF),
        ],
    )(even_layers, odd_layers, slices, *held_slices, base, *come_grads)
    weight_grads = call(last_kernel, [((4 + TAPS, width, lanes), F32)], [VMEM] * (1 + count))(
        sum_pieces, taps, *come_pieces
    )[0]
    return features_grad.reshape(features.shape), weight_grads.transpose(2, 0, 1)


def solution(mesh):
    token = P("azim", "sweep", "beam", None)
    in_specs = (token, token, P(), P(), P(), P(), P(), P())
    out_specs = (token, P("azim", None, ("beam", "sweep")))
    return jax.shard_map(per_device, mesh=mesh, in_specs=in_specs, out_specs=out_specs, check_vma=False)
```

```python
import functools

import jax
import jax.numpy as jnp
from jax import lax
from jax.experimental import pallas as pl
from jax.experimental.pallas import tpu as pltpu
from jax.sharding import PartitionSpec as P

HEADS = 8
SECTOR = 64
LANES = 128
TAPS = 27
MASKED = -1e30
GROUP = ("beam", "sweep")

NN = ((1,), (0,))
NT = ((1,), (1,))
TN = ((0,), (0,))

VMEM = pl.BlockSpec(memory_space=pltpu.VMEM)
HBM = pl.BlockSpec(memory_space=pltpu.HBM)
BF = jnp.bfloat16
F32 = jnp.float32


def dot(left, right, dims=NN):
    return lax.dot_general(left, right, (dims, ((), ())), preferred_element_type=F32)


def call(kernel, outs, in_specs, out_specs=None, scratch=(), aliases=None, limit=40, micros=2):
    return pl.pallas_call(
        kernel,
        cost_estimate=pl.CostEstimate(flops=int(micros * 1e9), bytes_accessed=0, transcendentals=0),
        out_shape=[jax.ShapeDtypeStruct(shape, dtype) for shape, dtype in outs],
        in_specs=in_specs,
        out_specs=out_specs or [VMEM] * len(outs),
        input_output_aliases=aliases or {},
        scratch_shapes=list(scratch),
        compiler_params=pltpu.CompilerParams(vmem_limit_bytes=limit << 20),
    )


def slot_of(other, own):
    differ = other ^ own
    return (differ & 1) * 4 + (differ >> 1)


def group_index():
    return lax.axis_index("beam") * lax.axis_size("sweep") + lax.axis_index("sweep")


def allowed_row(mask, count, keys):
    me = lax.axis_index("azim")
    square = mask.astype(F32)
    row = lax.broadcasted_iota(jnp.int32, square.shape, 0)
    own = jnp.sum(jnp.where(row == me, square, 0.0), axis=0, keepdims=True)
    sector = lax.broadcasted_iota(jnp.int32, (count, keys), 0)
    block = lax.broadcasted_iota(jnp.int32, (count, keys), 1) // SECTOR
    spread = jnp.where(sector == block ^ me, 1.0, 0.0).astype(BF)
    return dot(jnp.broadcast_to(own, (8, count)).astype(BF), spread)


def slices_kernel(even_ref, odd_ref, pieces_ref, slices_out, edges_out, pieces_out):
    pieces_out[...] = pieces_ref[...]
    me = group_index()
    _, beams, cols, channels = even_ref.shape
    width = channels // 8
    for side, col in enumerate((0, cols - 1)):
        base = col // 16 * 16
        rows = []
        for ref in (even_ref, odd_ref):
            for block in range(4):
                for b in range(beams):
                    part = ref[block, b, base : base + 16, :].astype(F32)
                    rows.append(part[col - base : col - base + 1])
        edges_out[side] = jnp.concatenate(rows, axis=0).astype(BF)
    channel = lax.broadcasted_iota(jnp.int32, (channels, 4 * width), 0) - width * me
    lane = lax.broadcasted_iota(jnp.int32, (channels, 4 * width), 1)
    total = [None] * 4
    for b in range(4):
        pick = jnp.where(channel + width * b == lane, 1.0, 0.0)
        pick = jnp.where((channel >= 0) & (channel < width), pick, 0.0).astype(BF)
        for s in range(4):
            slot = slot_of((b // beams) * 4 + s, me)
            odd = slot // 4
            block = lax.rem(slot, 4)
            value = jnp.where(odd == 1, odd_ref[block, b % beams], even_ref[block, b % beams])
            part = dot(value, pick)
            total[s] = part if total[s] is None else total[s] + part
    for s in range(4):
        slices_out[cols * s : cols * (s + 1), :] = total[s].astype(BF)


def neighbour_distances(count):
    return [distance for distance in range(1, count) if distance & (distance + 1) == 0]


def conv_kernel(count, even_ref, odd_ref, *refs):
    distances = neighbour_distances(count)
    edge_refs = refs[: len(distances)]
    w_ref, w_out_ref, layer_out, layer_bf_out, attended_out, main, edges, halo = refs[len(distances) :]
    me = group_index()
    column = lax.axis_index("azim")
    sweep = lax.axis_index("sweep")
    beam = lax.axis_index("beam")
    _, beams, cols, channels = even_ref.shape
    for index, step in enumerate((count - 1, 1)):
        partner = lax.rem(column + step, count) ^ column
        total = None
        for distance, ref in zip(distances, edge_refs):
            part = ref[1 - index].astype(F32) * jnp.where(partner == distance, 1.0, 0.0)
            total = part if total is None else total + part
        edges[index] = total
    for j in range(3):
        other_sweep = sweep + (j - 1)
        sweep_ok = (other_sweep >= 0) & (other_sweep < 4)
        for m in range(beams + 2):
            other_beam = beam + (-1 if m == 0 else (1 if m == beams + 1 else 0))
            within = (m - 1) % beams
            ok = sweep_ok & (other_beam >= 0) & (other_beam < 2)
            keep = jnp.where(ok, 1.0, 0.0)
            other = jnp.where(ok, other_beam * 4 + other_sweep, me)
            slot = slot_of(other, me)
            odd = slot // 4
            block = lax.rem(slot, 4)
            value = jnp.where(odd == 1, odd_ref[block, within], even_ref[block, within])
            main[j, m * cols : (m + 1) * cols, :] = (value.astype(F32) * keep).astype(BF)
            row = slot * beams + within
            for side in range(2):
                halo[side, j, m : m + 1, :] = edges[side, pl.ds(row, 1), :] * keep
    rows = beams * cols
    total = even_ref[0].reshape(rows, channels).astype(F32)
    spare = jnp.zeros((16 - beams, channels), F32)
    for i in (0, 1, -1):
        found = None
        for j in (-1, 0, 1):
            for k in (-1, 0, 1):
                left = main[1 - j, (1 - k) * cols : (1 - k + beams) * cols, :]
                if i:
                    edge = halo[0 if i == 1 else 1, 1 - j, 1 - k : 1 - k + beams, :]
                    left = jnp.concatenate([left, jnp.concatenate([edge, spare]).astype(BF)])
                part = dot(w_ref[9 * (i + 1) + 3 * (j + 1) + (k + 1)], left, NT)
                found = part if found is None else found + part
        found = found.T
        if i == 1:
            parts = [[found[rows + b : rows + b + 1], found[b * cols : (b + 1) * cols - 1]] for b in range(beams)]
        elif i == -1:
            parts = [[found[b * cols + 1 : (b + 1) * cols], found[rows + b : rows + b + 1]] for b in range(beams)]
        else:
            parts = [[found]]
        total = total + jnp.concatenate([part for pair in parts for part in pair], axis=0)
    rounded = total.astype(BF)
    layer_out[...] = total.reshape(beams, cols, channels)
    layer_bf_out[...] = rounded.reshape(beams, cols, channels)
    attended_out[...] = dot(rounded, w_out_ref[...], NT).astype(BF).reshape(beams, cols, channels)


def by_head(rows):
    cols, channels = rows.shape
    head = lax.broadcasted_iota(jnp.int32, rows.shape, 1) // (channels // HEADS)
    wide = rows.astype(F32)
    return jnp.concatenate([jnp.where(head == h, wide, 0.0).astype(BF) for h in range(HEADS)], axis=0)


def own_head(stacked):
    cols = stacked.shape[0] // HEADS
    channels = stacked.shape[1]
    head = lax.broadcasted_iota(jnp.int32, (cols, channels), 1) // (channels // HEADS)
    total = jnp.zeros((cols, channels), F32)
    for h in range(HEADS):
        total = jnp.where(head == h, stacked[h * cols : (h + 1) * cols], total)
    return total


def weights_of(queries_by_head, keys, allowed):
    scale = (queries_by_head.shape[1] // HEADS) ** (-0.5)
    scores = jnp.where(allowed, dot(queries_by_head, keys, NT) * scale, MASKED)
    peak = jnp.max(scores, axis=-1, keepdims=True)
    logsum = peak + jnp.log(jnp.sum(jnp.exp(scores - peak), axis=-1, keepdims=True))
    return jnp.where(allowed, jnp.exp(scores - logsum), 0.0)


def load_kernel(count, *refs):
    own_hbm, cot_hbm, mask_hbm, *weights_hbm = refs[:7]
    own_out, cot_out, allowed_out, *weights_out = refs[7:14]
    own, cot, mask, sems = refs[14:]
    copies = [
        pltpu.make_async_copy(source, target, sems.at[index])
        for index, (source, target) in enumerate(
            zip((own_hbm, cot_hbm, mask_hbm, *weights_hbm), (own, cot, mask, *weights_out))
        )
    ]
    for copy in copies:
        copy.start()
    for copy in copies:
        copy.wait()
    own_out[...] = jnp.swapaxes(own[...], 0, 1)
    cot_out[...] = jnp.swapaxes(cot[...], 0, 1)
    allowed_out[...] = allowed_row(mask[...], count, allowed_out.shape[1])


def project_kernel(count, *refs):
    own_ref, *come_refs = refs[:count]
    w_query, w_key, w_value, all_out, query_out, key_out, value_out = refs[count:]
    beams, cols, channels = own_ref.shape
    for distance in range(1, count):
        all_out[:, distance * cols : (distance + 1) * cols, :] = jnp.swapaxes(come_refs[distance - 1][...], 0, 1)
    all_out[:, :cols, :] = own_ref[...]
    every = all_out[...].reshape(beams * count * cols, channels)
    key_out[...] = dot(every, w_key[...]).astype(BF).reshape(beams, count * cols, channels)
    value_out[...] = dot(every, w_value[...]).astype(BF).reshape(beams, count * cols, channels)
    mine = all_out[:, :cols, :].reshape(beams * cols, channels)
    query_out[...] = dot(mine, w_query[...]).astype(BF).reshape(beams, cols, channels)


def stack_kernel(after_ref, own_ref, *refs):
    *come_refs, out = refs
    out[0] = own_ref[...]
    for index, ref in enumerate(come_refs, 1):
        out[index] = jnp.swapaxes(ref[...], 0, 1)


def attention_kernel(count, allowed_ref, all_ref, query_ref, key_ref, value_ref, w_out,
                     attended_out, pieces_out, weights_out):
    beams, cols, channels = query_ref.shape
    allowed = allowed_ref[0:1, :] > 0.5
    for b in range(beams):
        weights = weights_of(by_head(query_ref[b]), key_ref[b], allowed)
        weights_out[b] = weights
        attended_out[b] = own_head(dot(weights.astype(BF), value_ref[b])).astype(BF)
    own = all_ref[:, :cols, :].reshape(beams * cols, channels)
    mixed = own.astype(F32) + dot(attended_out[...].reshape(beams * cols, channels), w_out[...])
    me = lax.axis_index("azim")
    width = channels // count
    for owner in range(count):
        part = [mixed[b * cols : (b + 1) * cols, owner * width : (owner + 1) * width] for b in range(beams)]
        spare = pieces_out.shape[2] - beams * width
        if spare:
            part.append(jnp.zeros((cols, spare), F32))
        pieces_out[owner ^ me] = jnp.concatenate(part, axis=1).astype(BF)


def backward_kernel(count, weights_ref, all_ref, query_ref, key_ref, value_ref, attended_ref, grad_ref, layer_bf_ref,
                    layer_ref, w_query, w_key, w_value, base_out, send_out, keep_out, *refs):
    *pass_outs, grad_query, grad_key, grad_value, sums = refs
    beams, cols, channels = query_ref.shape
    scale = (channels // HEADS) ** (-0.5)
    for b in range(beams):
        queries = by_head(query_ref[b])
        keys = key_ref[b]
        weights = weights_ref[b]
        grads = by_head(grad_ref[b])
        attended = jnp.concatenate([attended_ref[b].astype(F32)] * HEADS, axis=0)
        delta = jnp.sum(grads.astype(F32) * attended, axis=-1, keepdims=True)
        grad_score = (weights * (dot(grads, value_ref[b], NT) - delta)).astype(BF)
        grad_query[b] = (own_head(dot(grad_score, keys)) * scale).astype(BF)
        grad_key[b] = (dot(grad_score, queries, TN) * scale).astype(BF)
        grad_value[b] = dot(weights.astype(BF), grads, TN).astype(BF)
    own_rows = beams * cols
    all_rows = beams * count * cols
    query_flat = grad_query[...].reshape(own_rows, channels)
    key_flat = grad_key[...].reshape(all_rows, channels)
    value_flat = grad_value[...].reshape(all_rows, channels)
    own = dot(query_flat, w_query[...], NT).reshape(beams, cols, channels) + layer_ref[...]
    spread = dot(key_flat, w_key[...], NT) + dot(value_flat, w_value[...], NT)
    spread = spread.reshape(beams, count, cols, channels)
    base_out[...] = own + spread[:, 0]
    for ahead in range(1, count):
        part = spread[:, ahead].astype(BF).reshape(beams * cols, channels)
        for half in range(channels // LANES):
            send_out[ahead - 1, half * beams * cols : (half + 1) * beams * cols, :] = part[
                :, half * LANES : (half + 1) * LANES
            ]
    every = all_ref[...].reshape(all_rows, channels)
    mine = all_ref[:, :cols, :].reshape(own_rows, channels)
    width = channels // 8
    for index, (left, right) in enumerate(
        (
            (query_flat, mine),
            (key_flat, every),
            (value_flat, every),
            (layer_bf_ref[...].reshape(own_rows, channels), attended_ref[...].reshape(own_rows, channels)),
        )
    ):
        sums[index] = dot(left, right, TN).astype(BF).reshape(8, width, channels)
    me = group_index()
    for differ in range(8):
        target = pass_outs[differ >> 1] if differ & 1 else keep_out.at[differ >> 1]
        for index in range(4):
            part = sums[index, me ^ differ]
            for half in range(channels // LANES):
                row = (half * 4 + index) * width
                target[row : row + width, :] = part[:, half * LANES : (half + 1) * LANES]


def pack_kernel(keep_ref, layer_ref, send_ref, give_ref, *refs):
    come_refs, give_outs, (send_out, give_out) = refs[:3], refs[3:6], refs[6:]
    rows = layer_ref.shape[0]
    for block, (ref, out) in enumerate(zip(come_refs, give_outs), 1):
        out[:rows, :] = layer_ref[...]
        out[rows:, :] = (keep_ref[block].astype(F32) + ref[...].astype(F32)).astype(BF)
    send_out[...] = send_ref[...]
    give_out[...] = give_ref[...]


def pieces_kernel(count, keep_ref, mine_ref, *refs):
    pieces_out = refs[-1]
    me = lax.axis_index("azim")
    rows = keep_ref.shape[1]
    total = keep_ref[0].astype(F32) + mine_ref[...].astype(F32)
    for ref in refs[:-1]:
        total = total + ref[ref.shape[0] - rows :, :].astype(F32)
    halves = 2
    rows = rows // halves
    total = jnp.concatenate([total[half * rows : (half + 1) * rows] for half in range(halves)], axis=1)
    width = total.shape[1] // count
    half = rows // 2
    for owner in range(count):
        part = total[:, owner * width : (owner + 1) * width]
        part = [part[:half], part[half:]]
        spare = pieces_out.shape[2] - 2 * width
        if spare:
            part.append(jnp.zeros((half, spare), F32))
        pieces_out[owner ^ me] = jnp.concatenate(part, axis=1).astype(BF)


def taps_kernel(count, even_ref, odd_ref, own_ref, *refs):
    packed_refs, base_ref, grad_refs = refs[: count - 1], refs[count - 1], refs[count : 2 * count - 1]
    taps_out, features_out, layers, turned, held = refs[2 * count - 1 :]
    beams, cols, channels = base_ref.shape
    rows = beams * cols
    total = base_ref[...].reshape(rows, channels)
    for ref in grad_refs:
        total = total + jnp.concatenate(
            [ref[half * rows : (half + 1) * rows, :].astype(F32) for half in range(channels // LANES)], axis=1
        )
    features_out[...] = jnp.swapaxes(total.reshape(beams, cols, channels).astype(BF), 0, 1)
    me = group_index()
    column = lax.axis_index("azim")
    lanes = taps_out.shape[2]
    width = taps_out.shape[1]
    per_sweep, rows = own_ref.shape[1], own_ref.shape[0] // 4
    held[0] = own_ref[...]
    for distance in range(1, count):
        ref = packed_refs[distance - 1]
        held[distance] = ref[ref.shape[0] - 4 * rows :, :]
    for s in range(4):
        for y in range(2):
            slot = slot_of(y * 4 + s, me)
            odd = slot // 4
            block = lax.rem(slot, 4)
            for owner in range(count):
                place = pl.ds(pl.multiple_of((owner ^ column) * rows, rows), rows)
                value = jnp.where(odd == 1, odd_ref[block, place, :], even_ref[block, place, :])
                layers[s, owner * rows : (owner + 1) * rows, y * 2 * lanes : (y + 1) * 2 * lanes] = value[:, : 2 * lanes]
    for s in range(4):
        cots = [held[owner ^ column, s * rows : (s + 1) * rows, :] for owner in range(count)]
        wide = jnp.concatenate(cots, axis=0).astype(F32).T
        for i in (-1, 0, 1):
            moved = wide if i == 0 else pltpu.roll(wide, i % wide.shape[1], 1)
            turned[i + 1, s * per_sweep : (s + 1) * per_sweep, :] = moved.astype(BF)
    for i in (-1, 0, 1):
        for j in (-1, 0, 1):
            found = None
            for s in range(4):
                if 0 <= s - j < 4:
                    part = dot(turned[i + 1, (s - j) * per_sweep : (s - j + 1) * per_sweep, :], layers[s])
                    found = part if found is None else found + part
            for k in (-1, 0, 1):
                tap = None
                for b in range(4):
                    if 0 <= b + k < 4:
                        part = found[b * width : (b + 1) * width, (b + k) * lanes : (b + k + 1) * lanes]
                        tap = part if tap is None else tap + part
                taps_out[9 * (i + 1) + 3 * (j + 1) + (k + 1)] = tap


def last_kernel(own_piece, taps_ref, *refs):
    *piece_refs, weights_out = refs
    piece = own_piece[0].astype(F32)
    for ref in piece_refs:
        piece = piece + ref[...].astype(F32)
    width, lanes = weights_out.shape[1:]
    for index in range(4):
        weights_out[index] = piece[
            (index % 2) * width : (index % 2 + 1) * width, (index // 2) * lanes : (index // 2 + 1) * lanes
        ]
    weights_out[4:] = taps_ref[...]


def in_hbm(value):
    return pltpu.with_memory_space_constraint(value, pltpu.HBM)


def swap_columns(value, distance):
    count = lax.axis_size("azim")
    return lax.ppermute(value, "azim", [(i, i ^ distance) for i in range(count)])


def exchange(values):
    come = {distance: swap_columns(values[distance], distance) for distance in sorted(values, reverse=True)}
    return [come[distance] for distance in sorted(values)]


def swap(value, bits):
    return lax.ppermute(value, GROUP, [(i, i ^ bits) for i in range(8)])


def per_device(features, cotangent, w_query, w_key, w_value, w_out, w_conv, sector_mask):
    cols, sweeps, beams, channels = features.shape
    count = lax.axis_size("azim")
    assert sweeps == 1 and beams == 2 and cols == SECTOR
    assert lax.axis_size("beam") == 2 and lax.axis_size("sweep") == 4
    width = channels // 8
    lanes = channels // count
    block = (beams, cols, channels)
    whole = (beams, count * cols, channels)

    token = (cols, beams, channels)
    square = (channels, channels)
    distances = range(1, count)
    raw_features, raw_cot = features.reshape(token), cotangent.reshape(token)
    come_features = exchange({distance: raw_features for distance in distances})
    come_cot = [swap(raw_cot, bits) for bits in (2, 4, 6)]

    own_features, own_cot, allowed, w_query, w_key, w_value, w_out = call(
        functools.partial(load_kernel, count),
        [(block, BF), (block, BF), ((8, count * cols), F32)] + [(square, BF)] * 4,
        [HBM] * 7,
        scratch=[pltpu.VMEM(token, BF)] * 2
        + [pltpu.VMEM(sector_mask.shape, jnp.int32), pltpu.SemaphoreType.DMA((7,))],
        micros=2,
    )(*map(in_hbm, (raw_features, raw_cot, sector_mask, w_query, w_key, w_value, w_out)))
    every, queries, keys, values = call(
        functools.partial(project_kernel, count),
        [(whole, BF), (block, BF), (whole, BF), (whole, BF)],
        [VMEM] * (count + 3),
        micros=0.01,
    )(own_features, *come_features, w_query, w_key, w_value)

    pieces_shape = (count, cols, max(LANES, beams * lanes))
    attended, pieces, weights = call(
        functools.partial(attention_kernel, count),
        [(block, BF), (pieces_shape, BF), ((beams, HEADS * cols, count * cols), F32)],
        [VMEM] * 6,
        micros=0.01,
    )(allowed, every, queries, keys, values, w_out)

    even = call(stack_kernel, [((4,) + block, BF)], [VMEM] * 5)(attended, own_cot, *come_cot)[0]
    odd = swap(even, 1)

    spread = (4 * cols, 4 * width)
    edge = (8 * beams, channels)
    slices, edges, pieces = call(
        slices_kernel, [(spread, BF), ((2,) + edge, BF), (pieces_shape, BF)], [VMEM] * 3
    )(even, odd, pieces)
    neighbours = exchange({distance: edges for distance in neighbour_distances(count)})

    far = count - 1
    packed = exchange(
        {
            distance: pieces[distance] if distance == far else jnp.concatenate([pieces[distance], slices])
            for distance in distances
        }
    )
    layer_block = jnp.concatenate([pieces[0]] + [part[:cols] for part in packed])

    grad_layer, grad_layer_bf, grad_attended = call(
        functools.partial(conv_kernel, count),
        [(block, F32), (block, BF), (block, BF)],
        [VMEM] * (4 + len(neighbours)),
        scratch=[
            pltpu.VMEM((3, (beams + 2) * cols, channels), BF),
            pltpu.VMEM((2,) + edge, F32),
            pltpu.VMEM((2, 3, 8, channels), F32),
        ],
    )(even, odd, *neighbours, w_conv.transpose(1, 0, 2), w_out)

    quarter = (4, 4 * width * channels // LANES, LANES)
    base, send, keep, *gives = call(
        functools.partial(backward_kernel, count),
        [(block, F32), ((count - 1, beams * cols * channels // LANES, LANES), BF), (quarter, BF)] + [(quarter[1:], BF)] * 4,
        [VMEM] * 12,
        scratch=[
            pltpu.VMEM(block, BF),
            pltpu.VMEM(whole, BF),
            pltpu.VMEM(whole, BF),
            pltpu.VMEM((4, 8, width, channels), BF),
        ],
    )(
        weights, every, queries, keys, values, attended, grad_attended, grad_layer_bf, grad_layer,
        w_query, w_key, w_value,
    )

    rows = quarter[1] + layer_block.shape[0]
    *packs, send, give = call(
        pack_kernel, [((rows, LANES), BF)] * 3 + [(send.shape, BF), (quarter[1:], BF)], [VMEM] * 7
    )(keep, layer_block, send, gives[0], *[swap(part, 1) for part in gives[1:]])
    mine = swap(give, 1)
    both = [swap(give, bits) for give, bits in zip(packs, (2, 4, 6))]
    relayed = packed[far - 2][cols:]
    come_grads = exchange(
        {
            distance: jnp.concatenate([send[distance - 1], relayed]) if distance == 1 else send[distance - 1]
            for distance in distances
        }
    )
    held_slices = packed[: far - 1] + [come_grads[0]]
    even_layers = jnp.stack([layer_block] + [part[: layer_block.shape[0]] for part in both])
    odd_layers = swap(even_layers, 1)
    sum_pieces = call(
        functools.partial(pieces_kernel, count),
        [((count, 2 * width, max(LANES, 2 * lanes)), BF)],
        [VMEM] * 5,
    )(keep, mine, *both)[0]
    come_pieces = exchange({distance: sum_pieces[distance] for distance in distances})

    taps, features_grad = call(
        functools.partial(taps_kernel, count),
        [((TAPS, width, lanes), F32), (token, BF)],
        [VMEM] * (2 + 2 * count),
        scratch=[
            pltpu.VMEM((4, count * cols, 4 * lanes), BF),
            pltpu.VMEM((3, 16 * width, count * cols), BF),
            pltpu.VMEM((count,) + spread, BF),
        ],
    )(even_layers, odd_layers, slices, *held_slices, base, *come_grads)
    weight_grads = call(last_kernel, [((4 + TAPS, width, lanes), F32)], [VMEM] * (1 + count))(
        sum_pieces, taps, *come_pieces
    )[0]
    return features_grad.reshape(features.shape), weight_grads.transpose(2, 0, 1)


def solution(mesh):
    token = P("azim", "sweep", "beam", None)
    in_specs = (token, token, P(), P(), P(), P(), P(), P())
    out_specs = (token, P("azim", None, ("beam", "sweep")))
    return jax.shard_map(per_device, mesh=mesh, in_specs=in_specs, out_specs=out_specs, check_vma=False)
```
